256 devices in a mesh: slab: 32 (over x, z_hi, core), blk: 8 (over z_lo, y).
Axes of the slice: x: 4, y: 4, z: 8 (z_hi: 4, z_lo: 2; z = z_hi * 2 + z_lo), core: 2. Of those that a mesh axis runs over, the one named last changes fastest.
Arguments:
- vectors: bfloat16 [147456, 3072], P('slab', 'blk'), may hold values from -0.25 to 0.25
- state_order: int32 [3072], P('blk'), may hold values from 0 to 383, as said below
Outputs:
- currents: float32 [4, 384, 3072], P(None, 'slab', 'blk')
The draws below stay inside these ranges and needn't reach their ends.
Inputs may be any that keep to these rules, and one draw needn't show every extreme that they name: `state_order`: each aligned run of 384 entries holds every number from 0 to 383 exactly once.
All inputs are finite; a program needn't handle non-finite values.
Results may differ from the reference program's by a relative error of at most 0.0031.
Values may be sent and summed in bfloat16 or wider, within the bound.
A program may use at most 128 MiB of HBM per device.

```python
import jax
import jax.numpy as jnp
from jax import lax

LX = 48
LY = 48
SB = 384
NZ = 64
S = 3072
NSITES = 147456
STEPS = 4
N_BLK = 8


def draw_state_order(key, part):
    key = jax.random.fold_in(key, 11)
    sub_keys = jax.random.split(key, S // SB)
    perms = jax.vmap(lambda sub_key: jax.random.permutation(sub_key, SB))(sub_keys)
    return perms.reshape(S).astype(jnp.int32)


def block_scale(stream_key, shape, pieces, least, high):
    factor_of, own = 1.0, jax.random.fold_in(stream_key, 6)
    for position, shards_of in pieces:
        steps = jnp.exp(jax.random.uniform(jax.random.fold_in(own, position), (shards_of,), jnp.float32, least / len(pieces), high / len(pieces)))
        factor_of = factor_of * jnp.repeat(steps, shape[position] // shards_of).reshape([-1 if axis == position else 1 for axis in range(len(shape))])
    return factor_of


def centred(own_key, shape, scale, bound, cuts=(), held_as=jnp.bfloat16):
    drawn = scale * jax.random.normal(own_key, shape, jnp.float32)
    if cuts:
        drawn = drawn * block_scale(own_key, shape, cuts, -0.22, 0.18)
    return jnp.clip(drawn, -bound, bound).astype(held_as)


def setup_inputs(seed: int = 0) -> dict:
    key_list = jax.random.split(jax.random.key(seed), 3)
    return {
        "vectors": centred(key_list[0], (NSITES, S), ((2 * NSITES) ** -0.25), 0.25, ((0, 32), (1, 8))),
        "state_order": draw_state_order(jax.random.fold_in(key_list[2], 71), 0),
    }


def reference(vectors, state_order):
    base = (jnp.arange(S, dtype=jnp.int32) // SB) * SB
    sorted_vec = jnp.take(vectors, base + state_order, axis=1)
    plane_stack = sorted_vec.reshape(NZ, LX * LY, S)

    def plane_image(z_index):
        upper_plane = plane_stack[(z_index + 1) % NZ].astype(jnp.float32)
        lower_plane = plane_stack[(z_index + NZ - 1) % NZ].astype(jnp.float32)
        return (upper_plane - lower_plane).astype(jnp.bfloat16)

    image_flat = lax.map(plane_image, jnp.arange(NZ, dtype=jnp.int32)).reshape(NSITES, S)

    def one_block(block_index):
        own_block = lax.dynamic_slice_in_dim(sorted_vec, block_index * SB, SB, 1)
        partner_cols = ((block_index + jnp.arange(STEPS, dtype=jnp.int32)[:, None]) % N_BLK) * SB + jnp.arange(SB, dtype=jnp.int32)[None, :]
        partner_image = jnp.take(image_flat, partner_cols.reshape(-1), axis=1)
        result = lax.dot_general(partner_image, own_block, (((0,), (0,)), ((), ())), preferred_element_type=jnp.float32)
        return result.reshape(STEPS, SB, SB)

    blocks = lax.map(one_block, jnp.arange(N_BLK, dtype=jnp.int32))
    return blocks.transpose(1, 2, 0, 3).reshape(STEPS, SB, S)
```

```python
import jax
import jax.numpy as jnp
from jax import lax
from jax.experimental import pallas as pl
from jax.experimental.pallas import tpu as pltpu
from jax.sharding import PartitionSpec as P

PLANE = 2304
QUARTER = 576
CHUNK = 1152
SB = 384
PIECE = 128
BF16 = jnp.bfloat16
F32 = jnp.float32
SENT = jnp.float32
MESH = pl.DeviceIdType.MESH
NEIGHBOURS = (3, 1, 2)


def kernel(
    vec, perm, out,
    w, u, halo, it, vn, part, xrecv, xsum, zrecv, fin, finr,
    swap_s, swap_r, pair_s, pair_r, outer_s, outer_r, sib_s, sib_r,
    y1_s, y1_r, y2_s, y2_r, x_s, x_r, z_s, z_r, fin_s, fin_r,
):
    slab, blk = lax.axis_index("slab"), lax.axis_index("blk")
    x, zh, c = slab // 8, (slab // 2) % 4, slab % 2
    zl, y = blk // 4, blk % 4
    keeper = c == zl

    def dev(x_, zh_, c_, zl_, y_):
        return (x_ * 8 + zh_ * 2 + c_, zl_ * 4 + y_)

    def remote(src, dst, ss, rs, where):
        return pltpu.make_async_remote_copy(
            src_ref=src, dst_ref=dst, send_sem=ss, recv_sem=rs,
            device_id=where, device_id_type=MESH,
        )

    zz = (x * 4 + zh) * 2 + zl
    zo = lax.rem(zz + 32 + 2 * zl - 1, 32)
    outer_dev = dev(zo // 8, (zo // 2) % 4, c, zo % 2, y)
    up = dev(x, zh, c, zl, (y + 1) % 4)
    down = dev(x, zh, c, zl, (y + 3) % 4)
    sibling = dev(x, zh, 1 - c, zl, y)

    swaps = [remote(w.at[j], u.at[j], swap_s.at[j], swap_r.at[j], dev(x, zh, zl, c, y)) for j in range(3)]
    pairs = [
        remote(w.at[j, :, :, 1 - c], halo.at[c, j], pair_s.at[j], pair_r.at[j], dev(x, zh, zl, 1 - c, y))
        for j in range(3)
    ]
    outers = [
        remote(u.at[j, :, :, zl], halo.at[1 - zl, j], outer_s.at[j], outer_r.at[j], outer_dev)
        for j in range(3)
    ]
    hop1 = [
        [remote(u.at[j, d], vn.at[d, j], y1_s.at[d, j], y1_r.at[d, j], (up, down)[d]) for d in range(2)]
        for j in range(3)
    ]
    hu = (((y + 1) % 4) // 2, ((y + 3) % 4) // 2)
    hop2 = [
        [remote(vn.at[d, j, hu[d]], vn.at[2, j, d], y2_s.at[d, j], y2_r.at[d, j], (up, down)[d]) for d in range(2)]
        for j in range(3)
    ]

    with jax.named_scope("sort"):
        row = lax.broadcasted_iota(jnp.int32, (SB, SB), 0)
        onehot = jnp.where(row == perm[...], 1.0, 0.0).astype(BF16)

        def sort_chunk(i, carry):
            plane, q = i // 4, i % 4
            at = pl.multiple_of(i * QUARTER, QUARTER)
            got = jnp.dot(vec[pl.ds(at, QUARTER), :], onehot, preferred_element_type=F32).astype(BF16)
            for j in range(3):
                w[j, q % 2, q // 2, plane] = got[:, j * PIECE:(j + 1) * PIECE]

            @pl.when(keeper)
            def _():
                for j in range(3):
                    u[j, q % 2, q // 2, plane] = got[:, j * PIECE:(j + 1) * PIECE]

            return carry

        lax.fori_loop(0, 8, sort_chunk, 0)

    @pl.when(jnp.logical_not(keeper))
    def _():
        for j in range(3):
            swaps[j].start()
        for j in range(3):
            pairs[j].start()

    for j in range(3):
        @pl.when(jnp.logical_not(keeper))
        def _():
            swaps[j].wait_recv()

        for d in range(2):
            hop1[j][d].start()
        outers[j].start()
        if j > 0:
            for d in range(2):
                hop1[j - 1][d].wait_recv()
                hop2[j - 1][d].start()
    for d in range(2):
        hop1[2][d].wait_recv()
        hop2[2][d].start()

    @pl.when(keeper)
    def _():
        for j in range(3):
            pairs[j].start()

    for j in range(3):
        outers[j].wait_recv()
        pairs[j].wait_recv()

    with jax.named_scope("image"):
        def image_chunk(i, carry):
            par, half = i // 2, i % 2
            for j in range(3):
                mine = u[j, par, half].astype(F32)
                first = mine[1] - halo[0, j, par, half].astype(F32)
                second = halo[1, j, par, half].astype(F32) - mine[0]
                both = jnp.concatenate([first, second], axis=0)
                it[c, par, half, j * PIECE:(j + 1) * PIECE, :] = both.astype(BF16).T
            return carry

        lax.fori_loop(0, 4, image_chunk, 0)
    sib = remote(it.at[c], it.at[c], sib_s, sib_r, sibling)
    sib.start()

    xsend = [
        [
            remote(part.at[t, :, (x + d) % 4], xrecv.at[t, d - 1], x_s.at[t, d - 1], x_r.at[t, d - 1],
                   dev((x + d) % 4, zh, c, zl, y))
            for d in (1, 2, 3)
        ]
        for t in range(7)
    ]

    def wide(ref):
        return jnp.concatenate([ref(j).reshape(CHUNK, PIECE) for j in range(3)], axis=1)

    def put(t, value):
        part[t] = value.reshape(3, 4, 32, SB).astype(SENT)
        for copy in xsend[t]:
            copy.start()

    with jax.named_scope("diagonal"):
        def own_chunk(i, total):
            par, half = i // 2, i % 2
            return total + jnp.dot(
                it[c, par, half], wide(lambda j: u[j, par, half]), preferred_element_type=F32
            )

        put(0, lax.fori_loop(0, 4, own_chunk, jnp.zeros((SB, SB), F32)))

    sib.wait_recv()
    where = [(c, y)]
    for i, n in enumerate(NEIGHBOURS):
        wraps = jnp.where(y + n >= 4, 1, 0)
        same = wraps * c + (1 - wraps) * (1 - c)
        where.append((c, (y + n) % 4))
        if n == 2:
            for j in range(3):
                for d in range(2):
                    hop2[j][d].wait_recv()

        for kind in range(2):
            who = same if kind == 0 else 1 - same

            def chunk(s, total, i=i, n=n, who=who):
                par, half = (s, y // 2) if n == 2 else ((0, s) if n == 3 else (1, s))
                return total + jnp.dot(
                    it[who, par, half], wide(lambda j: vn[i, j, s]), preferred_element_type=F32
                )

            got = lax.fori_loop(0, 2, chunk, jnp.zeros((SB, SB), F32))
            put(1 + i + 3 * kind, got if kind == 0 else -got.T)
    for i, n in enumerate(NEIGHBOURS):
        wraps = jnp.where(y + n >= 4, 1, 0)
        same = wraps * c + (1 - wraps) * (1 - c)
        where.append((1 - same, y))

    slots = [0] + [4 - n for n in NEIGHBOURS] + [3 + n for n in NEIGHBOURS]
    z8 = zh * 2 + zl
    for t in range(7):
        for copy in xsend[t]:
            copy.wait_recv()
        total = part[t, :, x].astype(F32)
        for d in range(3):
            total = total + xrecv[t, d].astype(F32)
        xsum[t] = total
        zp, yp = where[t]
        here = (zp == zl) & (yp == y) & keeper
        for h in range(4):
            is_self = here & (zh == h)

            @pl.when(is_self)
            def _():
                zrecv[slots[t], z8] = total[:, 8 * h:8 * h + 8]

            @pl.when(jnp.logical_not(is_self))
            def _():
                remote(xsum.at[t, :, 8 * h:8 * h + 8], zrecv.at[slots[t], z8], z_s.at[t], z_r.at[slots[t]],
                       dev(x, h, zp, zp, yp)).start()

    last = remote(fin, finr, fin_s, fin_r, sibling)

    def write(ref):
        for k in range(4):
            for j in range(3):
                rows = ref[k, j]
                out[k, 4 * j:4 * j + 4, :] = jnp.where(c == 0, rows[0:4], rows[4:8])

    @pl.when(keeper)
    def _():
        for s in range(7):
            if s == 0:
                few = y < 4
            elif s < 4:
                few = y > 4
            else:
                few = y + (s - 3) < 4

            @pl.when(few)
            def _():
                pltpu.make_async_copy(zrecv.at[s, 0:7], zrecv.at[s, 0:7], z_r.at[s]).wait()

            @pl.when(jnp.logical_not(few))
            def _():
                pltpu.make_async_copy(zrecv.at[s], zrecv.at[s], z_r.at[s]).wait()

        src = lax.broadcasted_iota(jnp.int32, (SB, SB), 0)
        dst = lax.broadcasted_iota(jnp.int32, (SB, SB), 1)
        slot = ((src % PIECE) // 4) * 12 + (src // PIECE) * 4 + src % 4
        unsort = jnp.where(slot == dst, 1.0, 0.0).astype(F32)
        for k in range(4):
            total = jnp.sum(zrecv[k], axis=0)
            if k > 0:
                total = total + jnp.sum(zrecv[3 + k], axis=0)
            flat = jnp.dot(total.reshape(24, SB), unsort, precision=lax.Precision.HIGHEST,
                           preferred_element_type=F32)
            fin[k] = flat.reshape(3, 8, SB)
        last.start()
        write(fin)
        last.wait_send()

    @pl.when(jnp.logical_not(keeper))
    def _():
        last.wait_recv()
        write(finr)
        for j in range(3):
            swaps[j].wait_send()

    for j in range(3):
        pairs[j].wait_send()
        outers[j].wait_send()
        for d in range(2):
            hop1[j][d].wait_send()
            hop2[j][d].wait_send()
    sib.wait_send()
    for t in range(7):
        for copy in xsend[t]:
            copy.wait_send()
        zp, yp = where[t]
        here = (zp == zl) & (yp == y) & keeper

        @pl.when(here)
        def _():
            pltpu.make_async_copy(xsum.at[t, :, 0:24], xsum.at[t, :, 0:24], z_s.at[t]).wait()

        @pl.when(jnp.logical_not(here))
        def _():
            pltpu.make_async_copy(xsum.at[t], xsum.at[t], z_s.at[t]).wait()


def on_device(vectors, state_order):
    perm = state_order.reshape(32, 3, 4).transpose(1, 0, 2).reshape(1, SB)
    dma = pltpu.SemaphoreType.DMA
    return pl.pallas_call(
        kernel,
        out_shape=jax.ShapeDtypeStruct((4, 12, SB), F32),
        in_specs=[pl.BlockSpec(memory_space=pltpu.VMEM)] * 2,
        out_specs=pl.BlockSpec(memory_space=pltpu.VMEM),
        scratch_shapes=[
            pltpu.VMEM((3, 2, 2, 2, QUARTER, PIECE), BF16),
            pltpu.VMEM((3, 2, 2, 2, QUARTER, PIECE), BF16),
            pltpu.VMEM((2, 3, 2, 2, QUARTER, PIECE), BF16),
            pltpu.VMEM((2, 2, 2, SB, CHUNK), BF16),
            pltpu.VMEM((3, 3, 2, 2, QUARTER, PIECE), BF16),
            pltpu.VMEM((7, 3, 4, 32, SB), SENT),
            pltpu.VMEM((7, 3, 3, 32, SB), SENT),
            pltpu.VMEM((7, 3, 32, SB), F32),
            pltpu.VMEM((7, 8, 3, 8, SB), F32),
            pltpu.VMEM((4, 3, 8, SB), F32),
            pltpu.VMEM((4, 3, 8, SB), F32),
            dma((3,)), dma((3,)), dma((3,)), dma((3,)), dma((3,)), dma((3,)),
            dma, dma,
            dma((2, 3)), dma((2, 3)), dma((2, 3)), dma((2, 3)),
            dma((7, 3)), dma((7, 3)), dma((7,)), dma((7,)),
            dma, dma,
        ],
        compiler_params=pltpu.CompilerParams(
            has_side_effects=True, vmem_limit_bytes=60 * 1024 * 1024
        ),
        cost_estimate=pl.CostEstimate(flops=6_000_000_000, bytes_accessed=4_000_000, transcendentals=0),
    )(vectors, perm)


def solution(mesh):
    return jax.shard_map(
        on_device,
        mesh=mesh,
        in_specs=(P("slab", "blk"), P("blk")),
        out_specs=P(None, "slab", "blk"),
        check_vma=False,
    )
```

```python
import jax
import jax.numpy as jnp
from jax import lax
from jax.experimental import pallas as pl
from jax.experimental.pallas import tpu as pltpu
from jax.sharding import PartitionSpec as P

PLANE = 2304
QUARTER = 576
CHUNK = 1152
SB = 384
PIECE = 128
BF16 = jnp.bfloat16
F32 = jnp.float32
SENT = jnp.bfloat16
MESH = pl.DeviceIdType.MESH
NEIGHBOURS = (3, 1, 2)


def kernel(
    vec_hbm, order, out,
    vec, w, u, halo, it, vn, part, xrecv, xsum, zrecv, fin, finr,
    swap_s, swap_r, pair_s, pair_r, outer_s, outer_r, sib_s, sib_r,
    y1_s, y1_r, y2_s, y2_r, x_s, x_r, z_s, z_r, fin_s, fin_r, load,
):
    slab, blk = lax.axis_index("slab"), lax.axis_index("blk")
    x, zh, c = slab // 8, (slab // 2) % 4, slab % 2
    zl, y = blk // 4, blk % 4
    keeper = c == zl

    def dev(x_, zh_, c_, zl_, y_):
        return (x_ * 8 + zh_ * 2 + c_, zl_ * 4 + y_)

    def remote(src, dst, ss, rs, where):
        return pltpu.make_async_remote_copy(
            src_ref=src, dst_ref=dst, send_sem=ss, recv_sem=rs,
            device_id=where, device_id_type=MESH,
        )

    zz = (x * 4 + zh) * 2 + zl
    zo = lax.rem(zz + 32 + 2 * zl - 1, 32)
    outer_dev = dev(zo // 8, (zo // 2) % 4, c, zo % 2, y)
    up = dev(x, zh, c, zl, (y + 1) % 4)
    down = dev(x, zh, c, zl, (y + 3) % 4)
    sibling = dev(x, zh, 1 - c, zl, y)

    fetch = pltpu.make_async_copy(vec_hbm, vec, load)
    fetch.start()
    barrier = pltpu.get_barrier_semaphore()

    def greet(where):
        pl.semaphore_signal(barrier, inc=1, device_id=where, device_id_type=MESH)

    me = blk * 8 + zh * 2 + c

    def greet_plane(i, carry):
        other = lax.rem(me + 1 + i, 64)
        greet((x * 8 + other % 8, other // 8))
        return carry

    lax.fori_loop(0, 63, greet_plane, 0)
    for d in (1, 2, 3):
        greet(dev((x + d) % 4, zh, c, zl, y))
    greet(outer_dev)

    swaps = [remote(w.at[j], u.at[j], swap_s.at[j], swap_r.at[j], dev(x, zh, zl, c, y)) for j in range(3)]
    pairs = [
        remote(w.at[j, :, :, 1 - c], halo.at[c, j], pair_s.at[j], pair_r.at[j], dev(x, zh, zl, 1 - c, y))
        for j in range(3)
    ]
    outers = [
        remote(u.at[j, :, :, zl], halo.at[1 - zl, j], outer_s.at[j], outer_r.at[j], outer_dev)
        for j in range(3)
    ]
    hop1 = [
        [remote(u.at[j, d], vn.at[d, j], y1_s.at[d, j], y1_r.at[d, j], (up, down)[d]) for d in range(2)]
        for j in range(3)
    ]
    hu = (((y + 1) % 4) // 2, ((y + 3) % 4) // 2)
    hop2 = [
        [remote(vn.at[d, j, hu[d]], vn.at[2, j, d], y2_s.at[d, j], y2_r.at[d, j], (up, down)[d]) for d in range(2)]
        for j in range(3)
    ]

    with jax.named_scope("sort"):
        row = lax.broadcasted_iota(jnp.int32, (SB, SB), 0)
        picked = jnp.where(row == order[...][None, :], 1.0, 0.0).astype(BF16)
        src = lax.broadcasted_iota(jnp.int32, (SB, SB), 0)
        dst = lax.broadcasted_iota(jnp.int32, (SB, SB), 1)
        slot = ((dst % PIECE) // 4) * 12 + (dst // PIECE) * 4 + dst % 4
        laid = jnp.where(slot == src, 1.0, 0.0).astype(BF16)
        onehot = jnp.dot(picked, laid, preferred_element_type=F32).astype(BF16)
        fetch.wait()

        def sort_chunk(i, carry):
            plane, q = i // 4, i % 4
            at = pl.multiple_of(i * QUARTER, QUARTER)
            got = jnp.dot(vec[pl.ds(at, QUARTER), :], onehot, preferred_element_type=F32).astype(BF16)
            for j in range(3):
                w[j, q % 2, q // 2, plane] = got[:, j * PIECE:(j + 1) * PIECE]

            @pl.when(keeper)
            def _():
                for j in range(3):
                    u[j, q % 2, q // 2, plane] = got[:, j * PIECE:(j + 1) * PIECE]

            return carry

        lax.fori_loop(0, 8, sort_chunk, 0)
    pl.semaphore_wait(barrier, 67)

    @pl.when(jnp.logical_not(keeper))
    def _():
        for j in range(3):
            swaps[j].start()
        for j in range(3):
            pairs[j].start()

    for j in range(3):
        @pl.when(jnp.logical_not(keeper))
        def _():
            swaps[j].wait_recv()

        for d in range(2):
            hop1[j][d].start()
        outers[j].start()
        if j > 0:
            for d in range(2):
                hop1[j - 1][d].wait_recv()
                hop2[j - 1][d].start()
    for d in range(2):
        hop1[2][d].wait_recv()
        hop2[2][d].start()

    @pl.when(keeper)
    def _():
        for j in range(3):
            pairs[j].start()

    for j in range(3):
        outers[j].wait_recv()
        pairs[j].wait_recv()

    with jax.named_scope("image"):
        def image_chunk(i, carry):
            par, half = i // 2, i % 2
            for j in range(3):
                mine = u[j, par, half].astype(F32)
                first = mine[1] - halo[0, j, par, half].astype(F32)
                second = halo[1, j, par, half].astype(F32) - mine[0]
                both = jnp.concatenate([first, second], axis=0)
                it[c, par, half, j * PIECE:(j + 1) * PIECE, :] = both.astype(BF16).T
            return carry

        lax.fori_loop(0, 4, image_chunk, 0)
    sib = remote(it.at[c], it.at[c], sib_s, sib_r, sibling)
    sib.start()

    xsend = [
        [
            remote(part.at[t, :, (x + d) % 4], xrecv.at[t, d - 1], x_s.at[t, d - 1], x_r.at[t, d - 1],
                   dev((x + d) % 4, zh, c, zl, y))
            for d in (1, 2, 3)
        ]
        for t in range(7)
    ]

    def wide(ref):
        return jnp.concatenate([ref(j).reshape(CHUNK, PIECE) for j in range(3)], axis=1)

    def put(t, value):
        part[t] = value.reshape(3, 4, 32, SB).astype(SENT)
        for copy in xsend[t]:
            copy.start()

    with jax.named_scope("diagonal"):
        def own_chunk(i, total):
            par, half = i // 2, i % 2
            return total + jnp.dot(
                it[c, par, half], wide(lambda j: u[j, par, half]), preferred_element_type=F32
            )

        put(0, lax.fori_loop(0, 4, own_chunk, jnp.zeros((SB, SB), F32)))

    sib.wait_recv()
    where = [(c, y)]
    for i, n in enumerate(NEIGHBOURS):
        wraps = jnp.where(y + n >= 4, 1, 0)
        same = wraps * c + (1 - wraps) * (1 - c)
        where.append((c, (y + n) % 4))
        if n == 2:
            for j in range(3):
                for d in range(2):
                    hop2[j][d].wait_recv()

        for kind in range(2):
            who = same if kind == 0 else 1 - same

            def chunk(s, total, i=i, n=n, who=who):
                par, half = (s, y // 2) if n == 2 else ((0, s) if n == 3 else (1, s))
                return total + jnp.dot(
                    it[who, par, half], wide(lambda j: vn[i, j, s]), preferred_element_type=F32
                )

            got = lax.fori_loop(0, 2, chunk, jnp.zeros((SB, SB), F32))
            put(1 + i + 3 * kind, got if kind == 0 else -got.T)
    for i, n in enumerate(NEIGHBOURS):
        wraps = jnp.where(y + n >= 4, 1, 0)
        same = wraps * c + (1 - wraps) * (1 - c)
        where.append((1 - same, y))

    slots = [0] + [4 - n for n in NEIGHBOURS] + [3 + n for n in NEIGHBOURS]
    z8 = zh * 2 + zl
    for t in range(7):
        for copy in xsend[t]:
            copy.wait_recv()
        total = part[t, :, x].astype(F32)
        for d in range(3):
            total = total + xrecv[t, d].astype(F32)
        xsum[t] = total
        zp, yp = where[t]
        here = (zp == zl) & (yp == y) & keeper
        for h in range(4):
            is_self = here & (zh == h)

            @pl.when(is_self)
            def _():
                zrecv[slots[t], z8] = total[:, 8 * h:8 * h + 8]

            @pl.when(jnp.logical_not(is_self))
            def _():
                remote(xsum.at[t, :, 8 * h:8 * h + 8], zrecv.at[slots[t], z8], z_s.at[t], z_r.at[slots[t]],
                       dev(x, h, zp, zp, yp)).start()

    last = remote(fin, finr, fin_s, fin_r, sibling)

    def write(ref):
        for k in range(4):
            for j in range(3):
                rows = ref[k, j]
                out[k, 4 * j:4 * j + 4, :] = jnp.where(c == 0, rows[0:4], rows[4:8])

    @pl.when(keeper)
    def _():
        for s in range(7):
            if s == 0:
                few = y < 4
            elif s < 4:
                few = y > 4
            else:
                few = y + (s - 3) < 4

            @pl.when(few)
            def _():
                pltpu.make_async_copy(zrecv.at[s, 0:7], zrecv.at[s, 0:7], z_r.at[s]).wait()

            @pl.when(jnp.logical_not(few))
            def _():
                pltpu.make_async_copy(zrecv.at[s], zrecv.at[s], z_r.at[s]).wait()

        src = lax.broadcasted_iota(jnp.int32, (SB, SB), 0)
        dst = lax.broadcasted_iota(jnp.int32, (SB, SB), 1)
        slot = ((src % PIECE) // 4) * 12 + (src // PIECE) * 4 + src % 4
        unsort = jnp.where(slot == dst, 1.0, 0.0).astype(F32)
        for k in range(4):
            total = jnp.sum(zrecv[k], axis=0)
            if k > 0:
                total = total + jnp.sum(zrecv[3 + k], axis=0)
            flat = jnp.dot(total.reshape(24, SB), unsort, precision=lax.Precision.HIGHEST,
                           preferred_element_type=F32)
            fin[k] = flat.reshape(3, 8, SB)
        last.start()
        write(fin)
        last.wait_send()

    @pl.when(jnp.logical_not(keeper))
    def _():
        last.wait_recv()
        write(finr)
        for j in range(3):
            swaps[j].wait_send()

    for j in range(3):
        pairs[j].wait_send()
        outers[j].wait_send()
        for d in range(2):
            hop1[j][d].wait_send()
            hop2[j][d].wait_send()
    sib.wait_send()
    for t in range(7):
        for copy in xsend[t]:
            copy.wait_send()
        zp, yp = where[t]
        here = (zp == zl) & (yp == y) & keeper

        @pl.when(here)
        def _():
            pltpu.make_async_copy(xsum.at[t, :, 0:24], xsum.at[t, :, 0:24], z_s.at[t]).wait()

        @pl.when(jnp.logical_not(here))
        def _():
            pltpu.make_async_copy(xsum.at[t], xsum.at[t], z_s.at[t]).wait()


def on_device(vectors, state_order):
    dma = pltpu.SemaphoreType.DMA
    return pl.pallas_call(
        kernel,
        out_shape=jax.ShapeDtypeStruct((4, 12, SB), F32),
        in_specs=[pl.BlockSpec(memory_space=pl.ANY), pl.BlockSpec(memory_space=pltpu.VMEM)],
        out_specs=pl.BlockSpec(memory_space=pltpu.VMEM),
        scratch_shapes=[
            pltpu.VMEM((2 * PLANE, SB), BF16),
            pltpu.VMEM((3, 2, 2, 2, QUARTER, PIECE), BF16),
            pltpu.VMEM((3, 2, 2, 2, QUARTER, PIECE), BF16),
            pltpu.VMEM((2, 3, 2, 2, QUARTER, PIECE), BF16),
            pltpu.VMEM((2, 2, 2, SB, CHUNK), BF16),
            pltpu.VMEM((3, 3, 2, 2, QUARTER, PIECE), BF16),
            pltpu.VMEM((7, 3, 4, 32, SB), SENT),
            pltpu.VMEM((7, 3, 3, 32, SB), SENT),
            pltpu.VMEM((7, 3, 32, SB), F32),
            pltpu.VMEM((7, 8, 3, 8, SB), F32),
            pltpu.VMEM((4, 3, 8, SB), F32),
            pltpu.VMEM((4, 3, 8, SB), F32),
            dma((3,)), dma((3,)), dma((3,)), dma((3,)), dma((3,)), dma((3,)),
            dma, dma,
            dma((2, 3)), dma((2, 3)), dma((2, 3)), dma((2, 3)),
            dma((7, 3)), dma((7, 3)), dma((7,)), dma((7,)),
            dma, dma, dma,
        ],
        compiler_params=pltpu.CompilerParams(
            collective_id=0, has_side_effects=True, vmem_limit_bytes=60 * 1024 * 1024
        ),
        cost_estimate=pl.CostEstimate(flops=6_000_000_000, bytes_accessed=4_000_000, transcendentals=0),
    )(vectors, state_order)


def solution(mesh):
    return jax.shard_map(
        on_device,
        mesh=mesh,
        in_specs=(P("slab", "blk"), P("blk")),
        out_specs=P(None, "slab", "blk"),
        check_vma=False,
    )
```

```python
import jax
import jax.numpy as jnp
from jax import lax
from jax.experimental import pallas as pl
from jax.experimental.pallas import tpu as pltpu
from jax.sharding import PartitionSpec as P

PLANE = 2304
QUARTER = 576
CHUNK = 1152
SB = 384
PIECE = 128
BF16 = jnp.bfloat16
F32 = jnp.float32
SENT = jnp.bfloat16
MESH = pl.DeviceIdType.MESH
NEIGHBOURS = (3, 1, 2)
TILE = {(2, 0): 2, (2, 1): 3, (0, 0): 4, (0, 1): 5, (1, 0): 6, (1, 1): 7, (0, 2): 8, (1, 2): 9}


def kernel(
    vec_hbm, order, out,
    vec, w, u, halo, it, vn, whole, part, xrecv, zsend, zrecv, fin, finr,
    swap_s, swap_r, pair_s, pair_r, outer_s, outer_r, sib_s, sib_r,
    y1_s, y1_r, y2_s, y2_r, x_s, x_r, z_s, z_r, fin_s, fin_r, load, sent,
):
    slab, blk = lax.axis_index("slab"), lax.axis_index("blk")
    x, zh, c = slab // 8, (slab // 2) % 4, slab % 2
    zl, y = blk // 4, blk % 4
    keeper = c == zl

    def dev(x_, zh_, c_, zl_, y_):
        return (x_ * 8 + zh_ * 2 + c_, zl_ * 4 + y_)

    def remote(src, dst, ss, rs, where):
        return pltpu.make_async_remote_copy(
            src_ref=src, dst_ref=dst, send_sem=ss, recv_sem=rs,
            device_id=where, device_id_type=MESH,
        )

    zz = (x * 4 + zh) * 2 + zl
    zo = lax.rem(zz + 32 + 2 * zl - 1, 32)
    outer_dev = dev(zo // 8, (zo // 2) % 4, c, zo % 2, y)
    up = dev(x, zh, c, zl, (y + 1) % 4)
    down = dev(x, zh, c, zl, (y + 3) % 4)
    sibling = dev(x, zh, 1 - c, zl, y)

    fetch = pltpu.make_async_copy(vec_hbm, vec, load)
    fetch.start()
    zrecv[:, :, 0:16] = jnp.zeros((7, 8, 16, PIECE), SENT)
    zrecv[:, :, 80:96] = jnp.zeros((7, 8, 16, PIECE), SENT)
    barrier = pltpu.get_barrier_semaphore()

    def greet(where):
        pl.semaphore_signal(barrier, inc=1, device_id=where, device_id_type=MESH)

    @pl.when(keeper)
    def _():
        me = zh * 8 + zl * 4 + y

        def greet_source(i, carry):
            other = lax.rem(me + 1 + i, 32)
            greet(dev(x, other // 8, c, (other // 4) % 2, other % 4))
            return carry

        def greet_crossing(i, carry):
            greet(dev(x, i // 2, 1 - c, i % 2, y))
            return carry

        lax.fori_loop(0, 31, greet_source, 0)
        lax.fori_loop(0, 8, greet_crossing, 0)

    @pl.when(jnp.logical_not(keeper))
    def _():
        def greet_owner(i, carry):
            greet(dev(x, i // 4, c, c, i % 4))
            return carry

        def greet_crossing(i, carry):
            greet(dev(x, i, 1 - c, 1 - c, y))
            return carry

        lax.fori_loop(0, 16, greet_owner, 0)
        lax.fori_loop(0, 4, greet_crossing, 0)
        greet(dev(x, zh, 1 - c, 1 - zl, y))
        greet(up)
        greet(down)

    for d in (1, 2, 3):
        greet(dev((x + d) % 4, zh, c, zl, y))
    greet(outer_dev)

    swap_dev = dev(x, zh, zl, c, y)
    swaps = [remote(w.at[j], u.at[j], swap_s.at[j], swap_r.at[j], swap_dev) for j in range(3)]
    pairs = [
        remote(w.at[j, :, :, 1 - c], halo.at[c, j], pair_s.at[j], pair_r.at[j], dev(x, zh, zl, 1 - c, y))
        for j in range(3)
    ]
    outers = [
        remote(u.at[j, :, :, zl], halo.at[1 - zl, j], outer_s.at[j], outer_r.at[j], outer_dev)
        for j in range(3)
    ]
    hop1 = [
        [remote(u.at[j, d], vn.at[d, j], y1_s.at[d, j], y1_r.at[d, j], (up, down)[d]) for d in range(2)]
        for j in range(3)
    ]
    hu = (((y + 1) % 4) // 2, ((y + 3) % 4) // 2)
    hop2 = [
        [remote(vn.at[d, j, hu[d]], vn.at[2, j, d], y2_s.at[d, j], y2_r.at[d, j], (up, down)[d]) for d in range(2)]
        for j in range(3)
    ]
    sib = [remote(it.at[c, j], it.at[c, j], sib_s.at[j], sib_r.at[j], sibling) for j in range(3)]

    def go(copies):
        for copy in copies:
            copy.start()

    def arrive(copies):
        for copy in copies:
            copy.wait_recv()

    with jax.named_scope("sort"):
        row = lax.broadcasted_iota(jnp.int32, (SB, SB), 0)
        picked = jnp.where(row == order[...][None, :], 1.0, 0.0).astype(BF16)
        src = lax.broadcasted_iota(jnp.int32, (SB, SB), 0)
        dst = lax.broadcasted_iota(jnp.int32, (SB, SB), 1)
        slot = ((dst % PIECE) // 4) * 12 + (dst // PIECE) * 4 + dst % 4
        laid = jnp.where(slot == src, 1.0, 0.0).astype(BF16)
        onehot = jnp.dot(picked, laid, preferred_element_type=F32).astype(BF16)
        fetch.wait()

        def sort_chunk(i, carry):
            plane, q = i // 4, i % 4
            at = pl.multiple_of(i * QUARTER, QUARTER)
            got = jnp.dot(vec[pl.ds(at, QUARTER), :], onehot, preferred_element_type=F32).astype(BF16)
            for j in range(3):
                w[j, q % 2, q // 2, plane] = got[:, j * PIECE:(j + 1) * PIECE]

            @pl.when(keeper)
            def _():
                for j in range(3):
                    u[j, q % 2, q // 2, plane] = got[:, j * PIECE:(j + 1) * PIECE]

            return carry

        lax.fori_loop(0, 8, sort_chunk, 0)
    pl.semaphore_wait(barrier, jnp.where(keeper, 43, 27))

    def image(lo, hi):
        def image_chunk(i, carry):
            par, half = i // 2, i % 2
            for j in range(lo, hi):
                mine = u[j, par, half].astype(F32)
                below = mine[1] - halo[0, j, par, half].astype(F32)
                above = halo[1, j, par, half].astype(F32) - mine[0]
                both = jnp.concatenate([below, above], axis=0)
                it[c, j, par, half] = both.astype(BF16).T
            return carry

        lax.fori_loop(0, 4, image_chunk, 0)

    def wide(pieces):
        return jnp.concatenate([piece.reshape(CHUNK, PIECE) for piece in pieces], axis=1)

    def product(n, who, rows, cols):
        def chunk(s, total):
            if n == 0:
                par, half = s // 2, s % 2
                right = wide([u[j, par, half] for j in cols])
            else:
                par, half = {1: (1, s), 2: (s, y // 2), 3: (0, s)}[n]
                right = wide([vn[NEIGHBOURS.index(n), j, s] for j in cols])
            left = jnp.concatenate([it[who, i, par, half] for i in rows], axis=0)
            return total + jnp.dot(left, right, preferred_element_type=F32)

        zero = jnp.zeros((PIECE * len(rows), PIECE * len(cols)), F32)
        return lax.fori_loop(0, 4 if n == 0 else 2, chunk, zero)

    def kind(t):
        if t == 0:
            return True, c, y, 0
        n, own = (t - 1) % 3 + 1, t < 4
        wraps = y + n >= 4
        matched = wraps if own else jnp.logical_not(wraps)
        zp = jnp.where(matched, c, c if own else 1 - c)
        yp = jnp.where(matched, (y + n) % 4, y)
        return matched, zp, yp, jnp.where(matched, 4 - n, 3 + n)

    def put(t, rows, cols, last):
        n = 0 if t == 0 else (t - 1) % 3 + 1
        got = product(n, c if t < 4 else 1 - c, rows, cols)
        matched = kind(t)[0]

        def tiles(swapped):
            for a, i in enumerate(rows):
                for b, j in enumerate(cols):
                    tile = got[a * PIECE:(a + 1) * PIECE, b * PIECE:(b + 1) * PIECE]
                    at = (j, i) if swapped else (i, j)
                    tile = -tile.T if swapped else tile
                    slot = last[int(swapped)] if at == (2, 2) else TILE[at]
                    whole[t, slot] = tile.reshape(4, 32, PIECE)
                    part[t, slot] = tile.reshape(4, 32, PIECE).astype(SENT)

        if t == 0:
            tiles(False)
            return
        pl.when(matched)(lambda: tiles(False))
        pl.when(jnp.logical_not(matched))(lambda: tiles(True))

    def xcopies(t, phase, start, length):
        run = pl.ds(start, length)
        return [
            remote(part.at[t, run, (x + d) % 4], xrecv.at[t, d - 1, run], x_s.at[t, phase, d - 1],
                   x_r.at[t, phase, d - 1], dev((x + d) % 4, zh, c, zl, y))
            for d in (1, 2, 3)
        ]

    z8 = zh * 2 + zl

    def collect(t, phase, start, length):
        arrive(xcopies(t, phase, start, length))
        run = pl.ds(start, length)
        total = whole[t, run, x]
        for d in range(3):
            total = total + xrecv[t, d, run].astype(F32)
        total = total.astype(SENT)
        rows = pl.ds(pl.multiple_of(8 * start, 16), 8 * length)
        _, zp, yp, slot = kind(t)
        here = (zp == zl) & (yp == y) & keeper
        for h in range(4):
            is_self = here & (zh == h)
            share = total[:, 8 * h:8 * h + 8].reshape(8 * length, PIECE)

            @pl.when(is_self)
            def _():
                zrecv[slot, z8, rows] = share

            @pl.when(jnp.logical_not(is_self))
            def _():
                zsend[t, h, rows] = share
                remote(zsend.at[t, h, rows], zrecv.at[slot, z8, rows], z_s.at[t], z_r.at[slot],
                       dev(x, h, zp, zp, yp)).start()

    def side(t, one, other):
        return jnp.where(kind(t)[0], one, other)

    def settle(copies):
        for copy in copies:
            copy.wait_send()

    def done(runs):
        for j in range(3):
            settle([outers[j], sib[j]] + hop1[j] + hop2[j])
        for run in runs:
            settle(xcopies(*run))
        for t in range(7):
            _, zp, yp, _ = kind(t)
            here = (zp == zl) & (yp == y) & keeper

            @pl.when(here)
            def _():
                pltpu.make_async_copy(zsend.at[t, 0:3, 0:80], zsend.at[t, 0:3, 0:80], z_s.at[t]).wait()

            @pl.when(jnp.logical_not(here))
            def _():
                pltpu.make_async_copy(zsend.at[t, :, 0:80], zsend.at[t, :, 0:80], z_s.at[t]).wait()

    final = remote(fin, finr, fin_s, fin_r, sibling)

    def write(ref):
        for k in range(4):
            for j in range(3):
                rows = ref[k, j]
                out[k, 4 * j:4 * j + 4, :] = jnp.where(c == 0, rows[0:4], rows[4:8])

    def keep():
        everything = (0, 1, 2)
        pairs[0].start()
        for j in range(3):
            go(hop1[j])
        go(outers)
        pairs[0].wait_send()
        pl.semaphore_signal(sent, inc=1, device_id=sibling, device_id_type=MESH)
        for j in range(3):
            arrive(hop1[j])
            go(hop2[j])

        def ready(j):
            arrive([pairs[j], outers[j]])
            image(j, j + 1)
            sib[j].start()

        ready(0)
        for j in range(3):
            arrive(hop2[j])
        pl.semaphore_wait(sent, 1)
        pairs[1].start()
        ready(1)
        runs = [(t, 0, side(t, 4, 2), 6) for t in range(7)]
        rest = [(t, 1, side(t, 0, 8), 4) for t in range(7)]

        def early(t):
            put(t, (0, 1), everything, (0, 0))
            go(xcopies(*runs[t]))

        def late(t):
            put(t, (2,), everything, (0, 10))
            go(xcopies(*rest[t]))

        for t in range(4):
            early(t)
        pairs[1].wait_send()
        pairs[2].start()
        ready(2)
        for t in range(4):
            late(t)
        for t in range(4):
            collect(*runs[t])
        arrive(sib[:2])
        for t in (4, 5, 6):
            early(t)
        for t in range(4):
            collect(*rest[t])
        arrive(sib[2:])
        for t in (4, 5, 6):
            late(t)
        for t in (4, 5, 6):
            collect(*runs[t])
        for t in (4, 5, 6):
            collect(*rest[t])

        for s in range(7):
            if s == 0:
                few = y < 4
            elif s < 4:
                few = y > 4
            else:
                few = y + (s - 3) < 4

            @pl.when(few)
            def _():
                pltpu.make_async_copy(zrecv.at[s, 0:7, 0:80], zrecv.at[s, 0:7, 0:80], z_r.at[s]).wait()

            @pl.when(jnp.logical_not(few))
            def _():
                pltpu.make_async_copy(zrecv.at[s, :, 0:80], zrecv.at[s, :, 0:80], z_r.at[s]).wait()

        src = lax.broadcasted_iota(jnp.int32, (SB, SB), 0)
        dst = lax.broadcasted_iota(jnp.int32, (SB, SB), 1)
        unsort = jnp.where(((src % PIECE) // 4) * 12 + (src // PIECE) * 4 + src % 4 == dst, 1.0, 0.0).astype(F32)
        for k in range(4):
            total = jnp.sum(zrecv[k].astype(F32), axis=0)
            if k > 0:
                total = total + jnp.sum(zrecv[3 + k].astype(F32), axis=0)
            at = [total[8 * i:8 * i + 8] for i in range(12)]
            flat = jnp.concatenate([
                jnp.concatenate([at[4], at[5], at[8]], axis=1),
                jnp.concatenate([at[6], at[7], at[9]], axis=1),
                jnp.concatenate([at[2], at[3], at[0] + at[10]], axis=1),
            ], axis=0)
            flat = jnp.dot(flat, unsort, precision=lax.Precision.HIGHEST, preferred_element_type=F32)
            fin[k] = flat.reshape(3, 8, SB)
        final.start()
        write(fin)
        final.wait_send()
        pairs[2].wait_send()
        done(runs + rest)

    def swap():
        everything = (0, 1, 2)
        def ready(j):
            arrive([pairs[j], outers[j]])
            image(j, j + 1)
            sib[j].start()

        go(pairs)
        swaps[0].start()
        pl.semaphore_wait(sent, 1)
        swaps[1].start()
        swaps[0].wait_send()
        swaps[2].start()
        swaps[0].wait_recv()
        go(hop1[0])
        outers[0].start()
        ready(0)
        swaps[1].wait_send()
        swaps[1].wait_recv()
        go(hop1[1])
        outers[1].start()
        arrive(hop1[0])
        go(hop2[0])
        swaps[2].wait_send()
        pl.semaphore_signal(sent, inc=1, device_id=sibling, device_id_type=MESH)
        swaps[2].wait_recv()
        go(hop1[2])
        outers[2].start()
        arrive(hop1[1])
        go(hop2[1])
        arrive(hop2[0])
        arrive(hop2[1])
        arrive(sib)
        runs = [(t, 0, 4, 4) for t in range(4)] + [(t, 0, side(t, 2, 4), 6) for t in (4, 5, 6)]
        for t in (4, 5, 6):
            put(t, everything, (0, 1), (0, 0))
            go(xcopies(*runs[t]))
        arrive(hop1[2])
        go(hop2[2])
        ready(1)
        for t in range(4):
            put(t, (0, 1), (0, 1), (0, 0))
            go(xcopies(*runs[t]))
        for t in (4, 5, 6):
            collect(*runs[t])
        arrive(hop2[2])
        rest = []
        for t in (4, 5, 6):
            put(t, everything, (2,), (10, 0))
            rest.append((t, 1, side(t, 8, 0), 4))
            go(xcopies(*rest[-1]))
        ready(2)
        for t in range(4):
            put(t, (2,), everything, (0, 0))
            put(t, (0, 1), (2,), (0, 0))
            rest += [(t, 1, 0, 4), (t, 2, 8, 2)]
            go(xcopies(*rest[-2]))
            go(xcopies(*rest[-1]))
        for t in range(4):
            collect(*runs[t])
        for run in rest:
            collect(*run)
        settle(pairs)
        done(runs + rest)
        final.wait_recv()
        write(finr)

    pl.when(keeper)(keep)
    pl.when(jnp.logical_not(keeper))(swap)


def on_device(vectors, state_order):
    dma = pltpu.SemaphoreType.DMA
    return pl.pallas_call(
        kernel,
        out_shape=jax.ShapeDtypeStruct((4, 12, SB), F32),
        in_specs=[pl.BlockSpec(memory_space=pl.ANY), pl.BlockSpec(memory_space=pltpu.VMEM)],
        out_specs=pl.BlockSpec(memory_space=pltpu.VMEM),
        scratch_shapes=[
            pltpu.VMEM((2 * PLANE, SB), BF16),
            pltpu.VMEM((3, 2, 2, 2, QUARTER, PIECE), BF16),
            pltpu.VMEM((3, 2, 2, 2, QUARTER, PIECE), BF16),
            pltpu.VMEM((2, 3, 2, 2, QUARTER, PIECE), BF16),
            pltpu.VMEM((2, 3, 2, 2, PIECE, CHUNK), BF16),
            pltpu.VMEM((3, 3, 2, 2, QUARTER, PIECE), BF16),
            pltpu.VMEM((7, 12, 4, 32, PIECE), F32),
            pltpu.VMEM((7, 12, 4, 32, PIECE), SENT),
            pltpu.VMEM((7, 3, 12, 32, PIECE), SENT),
            pltpu.VMEM((7, 4, 96, PIECE), SENT),
            pltpu.VMEM((7, 8, 96, PIECE), SENT),
            pltpu.VMEM((4, 3, 8, SB), F32),
            pltpu.VMEM((4, 3, 8, SB), F32),
            dma((3,)), dma((3,)), dma((3,)), dma((3,)), dma((3,)), dma((3,)),
            dma((3,)), dma((3,)),
            dma((2, 3)), dma((2, 3)), dma((2, 3)), dma((2, 3)),
            dma((7, 3, 3)), dma((7, 3, 3)), dma((7,)), dma((7,)),
            dma, dma, dma, pltpu.SemaphoreType.REGULAR,
        ],
        compiler_params=pltpu.CompilerParams(
            collective_id=0, has_side_effects=True, vmem_limit_bytes=60 * 1024 * 1024
        ),
        cost_estimate=pl.CostEstimate(flops=6_000_000_000, bytes_accessed=4_000_000, transcendentals=0),
    )(vectors, state_order)


def solution(mesh):
    return jax.shard_map(
        on_device,
        mesh=mesh,
        in_specs=(P("slab", "blk"), P("blk")),
        out_specs=P(None, "slab", "blk"),
        check_vma=False,
    )
```

```python
import jax
import jax.numpy as jnp
from jax import lax
from jax.experimental import pallas as pl
from jax.experimental.pallas import tpu as pltpu
from jax.sharding import PartitionSpec as P

PLANE = 2304
QUARTER = 576
CHUNK = 1152
SB = 384
PIECE = 128
BF16 = jnp.bfloat16
F32 = jnp.float32
SENT = jnp.bfloat16
MESH = pl.DeviceIdType.MESH
NEIGHBOURS = (3, 1, 2)
TILE = {(0, 0): 2, (0, 1): 3, (1, 0): 4, (1, 1): 5, (0, 2): 6, (1, 2): 7, (2, 2): 8}


def kernel(
    vec_hbm, order, out,
    vec, w, u, halo, it, vn, whole, part, xrecv, zsend, zrecv, fin, finr, layout,
    swap_s, swap_r, pair_s, pair_r, outer_s, outer_r, sib_s, sib_r,
    y1_s, y1_r, y2_s, y2_r, x_s, x_r, z_s, z_r, fin_s, fin_r, load, sent,
):
    slab, blk = lax.axis_index("slab"), lax.axis_index("blk")
    x, zh, c = slab // 8, (slab // 2) % 4, slab % 2
    zl, y = blk // 4, blk % 4
    keeper = c == zl

    def dev(x_, zh_, c_, zl_, y_):
        return (x_ * 8 + zh_ * 2 + c_, zl_ * 4 + y_)

    def remote(src, dst, ss, rs, where):
        return pltpu.make_async_remote_copy(
            src_ref=src, dst_ref=dst, send_sem=ss, recv_sem=rs,
            device_id=where, device_id_type=MESH,
        )

    zz = (x * 4 + zh) * 2 + zl
    zo = lax.rem(zz + 32 + 2 * zl - 1, 32)
    outer_dev = dev(zo // 8, (zo // 2) % 4, c, zo % 2, y)
    up = dev(x, zh, c, zl, (y + 1) % 4)
    down = dev(x, zh, c, zl, (y + 3) % 4)
    sibling = dev(x, zh, 1 - c, zl, y)

    fetch = pltpu.make_async_copy(vec_hbm, vec, load)
    fetch.start()
    zrecv[:, :, 0:16] = jnp.zeros((7, 8, 16, PIECE), SENT)
    zrecv[:, :, 80:96] = jnp.zeros((7, 8, 16, PIECE), SENT)
    barrier = pltpu.get_barrier_semaphore()

    def greet(where):
        pl.semaphore_signal(barrier, inc=1, device_id=where, device_id_type=MESH)

    @pl.when(keeper)
    def _():
        me = zh * 8 + zl * 4 + y

        def greet_source(i, carry):
            other = lax.rem(me + 1 + i, 32)
            greet(dev(x, other // 8, c, (other // 4) % 2, other % 4))
            return carry

        def greet_crossing(i, carry):
            greet(dev(x, i // 2, 1 - c, i % 2, y))
            return carry

        lax.fori_loop(0, 31, greet_source, 0)
        lax.fori_loop(0, 8, greet_crossing, 0)

    @pl.when(jnp.logical_not(keeper))
    def _():
        def greet_owner(i, carry):
            greet(dev(x, i // 4, c, c, i % 4))
            return carry

        def greet_crossing(i, carry):
            greet(dev(x, i, 1 - c, 1 - c, y))
            return carry

        lax.fori_loop(0, 16, greet_owner, 0)
        lax.fori_loop(0, 4, greet_crossing, 0)
        greet(dev(x, zh, 1 - c, 1 - zl, y))
        greet(up)
        greet(down)

    for d in (1, 2, 3):
        greet(dev((x + d) % 4, zh, c, zl, y))
    greet(outer_dev)

    swap_dev = dev(x, zh, zl, c, y)
    swaps = [remote(w.at[j], u.at[j], swap_s.at[j], swap_r.at[j], swap_dev) for j in range(3)]
    pairs = [
        remote(w.at[j, :, :, 1 - c], halo.at[c, j], pair_s.at[j], pair_r.at[j], dev(x, zh, zl, 1 - c, y))
        for j in range(3)
    ]
    outers = [
        remote(u.at[j, :, :, zl], halo.at[1 - zl, j], outer_s.at[j], outer_r.at[j], outer_dev)
        for j in range(3)
    ]
    on = ((y + 2) % 4) // 2
    hop1 = [
        [
            remote(u.at[j, d, half], vn.at[d, j, half], y1_s.at[d, j, part_], y1_r.at[d, j, part_], (up, down)[d])
            for part_, half in enumerate((on, 1 - on)) for d in range(2)
        ]
        for j in range(3)
    ]
    hu = (((y + 1) % 4) // 2, ((y + 3) % 4) // 2)
    hop2 = [
        [remote(vn.at[d, j, hu[d]], vn.at[2, j, d], y2_s.at[d, j], y2_r.at[d, j], (up, down)[d]) for d in range(2)]
        for j in range(3)
    ]
    sib = [remote(it.at[c, j], it.at[c, j], sib_s.at[j], sib_r.at[j], sibling) for j in range(3)]

    def go(copies):
        for copy in copies:
            copy.start()

    def arrive(copies):
        for copy in copies:
            copy.wait_recv()

    with jax.named_scope("sort"):
        row = lax.broadcasted_iota(jnp.int32, (SB, SB), 0)
        picked = jnp.where(row == order[...][None, :], 1.0, 0.0).astype(BF16)
        src = lax.broadcasted_iota(jnp.int32, (SB, SB), 0)
        dst = lax.broadcasted_iota(jnp.int32, (SB, SB), 1)
        slot = ((dst % PIECE) // 4) * 12 + (dst // PIECE) * 4 + dst % 4
        laid = jnp.where(slot == src, 1.0, 0.0).astype(BF16)
        layout[...] = laid
        onehot = jnp.dot(picked, laid, preferred_element_type=F32).astype(BF16)
        fetch.wait()

        def sort_chunk(i, carry):
            plane, q = i // 4, i % 4
            at = pl.multiple_of(i * QUARTER, QUARTER)
            got = jnp.dot(vec[pl.ds(at, QUARTER), :], onehot, preferred_element_type=F32).astype(BF16)
            for j in range(3):
                w[j, q % 2, q // 2, plane] = got[:, j * PIECE:(j + 1) * PIECE]

            @pl.when(keeper)
            def _():
                for j in range(3):
                    u[j, q % 2, q // 2, plane] = got[:, j * PIECE:(j + 1) * PIECE]

            return carry

        lax.fori_loop(0, 8, sort_chunk, 0)
    pl.semaphore_wait(barrier, jnp.where(keeper, 43, 27))

    def image(lo, hi):
        def image_chunk(i, carry):
            par, half = i // 2, i % 2
            for j in range(lo, hi):
                mine = u[j, par, half].astype(F32)
                below = mine[1] - halo[0, j, par, half].astype(F32)
                above = halo[1, j, par, half].astype(F32) - mine[0]
                both = jnp.concatenate([below, above], axis=0)
                it[c, j, par, half] = both.astype(BF16).T
            return carry

        lax.fori_loop(0, 4, image_chunk, 0)

    def wide(pieces):
        return jnp.concatenate([piece.reshape(CHUNK, PIECE) for piece in pieces], axis=1)

    def product(n, who, rows, cols):
        if n == 0:
            steps = [(s // 2, s % 2) for s in range(4)]
            right = [wide([u[j, par, half] for j in cols]) for par, half in steps]
        else:
            steps = [{1: (1, s), 2: (s, y // 2), 3: (0, s)}[n] for s in range(2)]
            right = [wide([vn[NEIGHBOURS.index(n), j, s] for j in cols]) for s in range(2)]
        left = [jnp.concatenate([it[who, i, par, half] for i in rows], axis=0) for par, half in steps]
        return jnp.dot(
            jnp.concatenate(left, axis=1), jnp.concatenate(right, axis=0), preferred_element_type=F32
        )

    def kind(t):
        if t == 0:
            return True, c, y, 0
        n, own = (t - 1) % 3 + 1, t < 4
        wraps = y + n >= 4
        matched = wraps if own else jnp.logical_not(wraps)
        zp = jnp.where(matched, c, c if own else 1 - c)
        yp = jnp.where(matched, (y + n) % 4, y)
        return matched, zp, yp, jnp.where(matched, 4 - n, 3 + n)

    def put(t, rows, cols, early):
        n = 0 if t == 0 else (t - 1) % 3 + 1
        got = product(n, c if t < 4 else 1 - c, rows, cols)
        matched = kind(t)[0]

        def tiles(swapped):
            for a, i in enumerate(rows):
                for b, j in enumerate(cols):
                    tile = got[a * PIECE:(a + 1) * PIECE, b * PIECE:(b + 1) * PIECE]
                    at = (j, i) if swapped else (i, j)
                    tile = -tile.T if swapped else tile
                    slot = TILE[at] if at in TILE else at[1] + (0 if early else 10)
                    whole[t, slot] = tile.reshape(4, 32, PIECE)
                    part[t, slot] = tile.reshape(4, 32, PIECE).astype(SENT)

        if t == 0:
            tiles(False)
            return
        pl.when(matched)(lambda: tiles(False))
        pl.when(jnp.logical_not(matched))(lambda: tiles(True))

    def xcopies(t, phase, start, length):
        run = pl.ds(start, length)
        return [
            remote(part.at[t, run, (x + d) % 4], xrecv.at[t, d - 1, run], x_s.at[t, phase, d - 1],
                   x_r.at[t, phase, d - 1], dev((x + d) % 4, zh, c, zl, y))
            for d in (1, 2, 3)
        ]

    z8 = zh * 2 + zl

    def collect(t, phase, start, length):
        arrive(xcopies(t, phase, start, length))
        run = pl.ds(start, length)
        total = whole[t, run, x]
        for d in range(3):
            total = total + xrecv[t, d, run].astype(F32)
        total = total.astype(SENT)
        rows = pl.ds(pl.multiple_of(8 * start, 16), 8 * length)
        _, zp, yp, slot = kind(t)
        here = (zp == zl) & (yp == y) & keeper
        for h in range(4):
            zsend[t, h, rows] = total[:, 8 * h:8 * h + 8].reshape(8 * length, PIECE)
            copy = remote(zsend.at[t, h, rows], zrecv.at[slot, z8, rows], z_s.at[t], z_r.at[slot], dev(x, h, zp, zp, yp))
            pl.when(jnp.logical_not(here & (zh == h)))(copy.start)

        @pl.when(here)
        def _():
            zrecv[slot, z8, rows] = zsend[t, zh, rows]

    def side(t, one, other):
        return jnp.where(kind(t)[0], one, other)

    def pass_on(j):
        for d in range(2):
            hop1[j][d].wait_recv()
            hop2[j][d].start()

    def all_here(j):
        arrive(hop1[j][2:])
        arrive(hop2[j])

    def settle(copies):
        for copy in copies:
            copy.wait_send()

    def done(runs):
        for j in range(3):
            settle([outers[j], sib[j]] + hop1[j] + hop2[j])
        for run in runs:
            settle(xcopies(*run))
        for t in range(7):
            _, zp, yp, _ = kind(t)
            here = (zp == zl) & (yp == y) & keeper

            @pl.when(here)
            def _():
                pltpu.make_async_copy(zsend.at[t, 0:3, 0:80], zsend.at[t, 0:3, 0:80], z_s.at[t]).wait()

            @pl.when(jnp.logical_not(here))
            def _():
                pltpu.make_async_copy(zsend.at[t, :, 0:80], zsend.at[t, :, 0:80], z_s.at[t]).wait()

    final = remote(fin, finr, fin_s, fin_r, sibling)

    def write(ref):
        for k in range(4):
            for j in range(3):
                rows = ref[k, j]
                out[k, 4 * j:4 * j + 4, :] = jnp.where(c == 0, rows[0:4], rows[4:8])

    def keep():
        everything = (0, 1, 2)
        pairs[0].start()
        for j in range(3):
            go(hop1[j])
        go(outers)
        pairs[0].wait_send()
        pl.semaphore_signal(sent, inc=1, device_id=sibling, device_id_type=MESH)
        for j in range(3):
            pass_on(j)

        def ready(j):
            arrive([pairs[j], outers[j]])
            image(j, j + 1)
            sib[j].start()

        ready(0)
        for j in range(3):
            all_here(j)
        pl.semaphore_wait(sent, 1)
        pairs[1].start()
        ready(1)
        runs = [(t, 0, side(t, 2, 0), 6) for t in range(7)]
        rest = [(t, 1, side(t, 8, 6), 4) for t in range(7)]

        def early(t):
            put(t, (0, 1), everything, True)
            go(xcopies(*runs[t]))

        def late(t):
            put(t, (2,), everything, False)
            go(xcopies(*rest[t]))

        for t in range(4):
            early(t)
        pairs[1].wait_send()
        pairs[2].start()
        ready(2)
        for t in range(4):
            late(t)
        for t in range(4):
            collect(*runs[t])
        arrive(sib[:2])
        for t in (4, 5, 6):
            early(t)
        for t in range(4):
            collect(*rest[t])
        arrive(sib[2:])
        for t in (4, 5, 6):
            late(t)
        for t in (4, 5, 6):
            collect(*runs[t])
        for t in (4, 5, 6):
            collect(*rest[t])

        for s in range(7):
            if s == 0:
                few = y < 4
            elif s < 4:
                few = y > 4
            else:
                few = y + (s - 3) < 4

            @pl.when(few)
            def _():
                pltpu.make_async_copy(zrecv.at[s, 0:7, 0:80], zrecv.at[s, 0:7, 0:80], z_r.at[s]).wait()

            @pl.when(jnp.logical_not(few))
            def _():
                pltpu.make_async_copy(zrecv.at[s, :, 0:80], zrecv.at[s, :, 0:80], z_r.at[s]).wait()

        flats = []
        for k in range(4):
            total = jnp.sum(zrecv[k].astype(F32), axis=0)
            if k > 0:
                total = total + jnp.sum(zrecv[3 + k].astype(F32), axis=0)
            at = [total[8 * i:8 * i + 8] for i in range(12)]
            flats += [
                jnp.concatenate([at[2], at[3], at[6]], axis=1),
                jnp.concatenate([at[4], at[5], at[7]], axis=1),
                jnp.concatenate([at[0] + at[10], at[1] + at[11], at[8]], axis=1),
            ]
        flat = jnp.concatenate(flats, axis=0)
        high = flat.astype(BF16)
        left = flat - high.astype(F32)
        middle = left.astype(BF16)
        low = (left - middle.astype(F32)).astype(BF16)
        flat = lax.dot_general(
            jnp.concatenate([high, middle, low], axis=0), layout[...], (((1,), (1,)), ((), ())),
            preferred_element_type=F32,
        )
        flat = flat[0:96] + flat[96:192] + flat[192:288]
        fin[...] = flat.reshape(4, 3, 8, SB)
        final.start()
        write(fin)
        final.wait_send()
        pairs[2].wait_send()
        done(runs + rest)

    def swap():
        everything = (0, 1, 2)
        def ready(j):
            arrive([pairs[j], outers[j]])
            image(j, j + 1)
            sib[j].start()

        go(pairs)
        swaps[0].start()
        pl.semaphore_wait(sent, 1)
        swaps[1].start()
        swaps[0].wait_send()
        swaps[2].start()
        swaps[0].wait_recv()
        go(hop1[0])
        outers[0].start()
        ready(0)
        pass_on(0)
        swaps[1].wait_send()
        swaps[1].wait_recv()
        go(hop1[1])
        outers[1].start()
        pass_on(1)
        swaps[2].wait_send()
        pl.semaphore_signal(sent, inc=1, device_id=sibling, device_id_type=MESH)
        swaps[2].wait_recv()
        go(hop1[2])
        outers[2].start()
        pass_on(2)
        all_here(0)
        all_here(1)
        runs = [(t, 0, 2, 4) for t in range(4)] + [(t, 0, side(t, 0, 2), 6) for t in (4, 5, 6)]
        ready(1)
        for t in range(4):
            put(t, (0, 1), (0, 1), True)
            go(xcopies(*runs[t]))
        arrive(sib)
        for t in (4, 5, 6):
            put(t, everything, (0, 1), True)
            go(xcopies(*runs[t]))
        for t in range(4):
            collect(*runs[t])
        all_here(2)
        rest = []
        for t in (4, 5, 6):
            put(t, everything, (2,), False)
            rest.append((t, 1, side(t, 6, 8), 4))
            go(xcopies(*rest[-1]))
        ready(2)
        for t in range(4):
            put(t, (2,), everything, False)
            put(t, (0, 1), (2,), False)
            rest.append((t, 1, 6, 6))
            go(xcopies(*rest[-1]))
        for run in runs[4:] + rest:
            collect(*run)
        settle(pairs)
        done(runs + rest)
        final.wait_recv()
        write(finr)

    pl.when(keeper)(keep)
    pl.when(jnp.logical_not(keeper))(swap)


def on_device(vectors, state_order):
    dma = pltpu.SemaphoreType.DMA
    return pl.pallas_call(
        kernel,
        out_shape=jax.ShapeDtypeStruct((4, 12, SB), F32),
        in_specs=[pl.BlockSpec(memory_space=pl.ANY), pl.BlockSpec(memory_space=pltpu.VMEM)],
        out_specs=pl.BlockSpec(memory_space=pltpu.VMEM),
        scratch_shapes=[
            pltpu.VMEM((2 * PLANE, SB), BF16),
            pltpu.VMEM((3, 2, 2, 2, QUARTER, PIECE), BF16),
            pltpu.VMEM((3, 2, 2, 2, QUARTER, PIECE), BF16),
            pltpu.VMEM((2, 3, 2, 2, QUARTER, PIECE), BF16),
            pltpu.VMEM((2, 3, 2, 2, PIECE, CHUNK), BF16),
            pltpu.VMEM((3, 3, 2, 2, QUARTER, PIECE), BF16),
            pltpu.VMEM((7, 12, 4, 32, PIECE), F32),
            pltpu.VMEM((7, 12, 4, 32, PIECE), SENT),
            pltpu.VMEM((7, 3, 12, 32, PIECE), SENT),
            pltpu.VMEM((7, 4, 96, PIECE), SENT),
            pltpu.VMEM((7, 8, 96, PIECE), SENT),
            pltpu.VMEM((4, 3, 8, SB), F32),
            pltpu.VMEM((4, 3, 8, SB), F32),
            pltpu.VMEM((SB, SB), BF16),
            dma((3,)), dma((3,)), dma((3,)), dma((3,)), dma((3,)), dma((3,)),
            dma((3,)), dma((3,)),
            dma((2, 3, 2)), dma((2, 3, 2)), dma((2, 3)), dma((2, 3)),
            dma((7, 3, 3)), dma((7, 3, 3)), dma((7,)), dma((7,)),
            dma, dma, dma, pltpu.SemaphoreType.REGULAR,
        ],
        compiler_params=pltpu.CompilerParams(
            collective_id=0, has_side_effects=True, vmem_limit_bytes=60 * 1024 * 1024
        ),
        cost_estimate=pl.CostEstimate(flops=6_000_000_000, bytes_accessed=4_000_000, transcendentals=0),
    )(vectors, state_order)


def solution(mesh):
    return jax.shard_map(
        on_device,
        mesh=mesh,
        in_specs=(P("slab", "blk"), P("blk")),
        out_specs=P(None, "slab", "blk"),
        check_vma=False,
    )
```

```python
import jax
import jax.numpy as jnp
from jax import lax
from jax.experimental import pallas as pl
from jax.experimental.pallas import tpu as pltpu
from jax.sharding import PartitionSpec as P

PLANE = 2304
QUARTER = 576
CHUNK = 1152
SB = 384
PIECE = 128
BF16 = jnp.bfloat16
F32 = jnp.float32
SENT = jnp.bfloat16
MESH = pl.DeviceIdType.MESH
NEIGHBOURS = (3, 1, 2)
TILE = {(0, 0): 2, (0, 1): 3, (1, 0): 4, (1, 1): 5, (0, 2): 6, (1, 2): 7, (2, 2): 8}


def kernel(
    vec_hbm, order, out,
    vec, w, u, halo, it, vn, whole, part, xrecv, zsend, zrecv, fin, finr, layout,
    swap_s, swap_r, pair_s, pair_r, outer_s, outer_r, sib_s, sib_r,
    y1_s, y1_r, y2_s, y2_r, x_s, x_r, z_s, z_r, fin_s, fin_r, load, sent,
):
    slab, blk = lax.axis_index("slab"), lax.axis_index("blk")
    x, zh, c = slab // 8, (slab // 2) % 4, slab % 2
    zl, y = blk // 4, blk % 4
    keeper = c == zl

    def dev(x_, zh_, c_, zl_, y_):
        return (x_ * 8 + zh_ * 2 + c_, zl_ * 4 + y_)

    def remote(src, dst, ss, rs, where):
        return pltpu.make_async_remote_copy(
            src_ref=src, dst_ref=dst, send_sem=ss, recv_sem=rs,
            device_id=where, device_id_type=MESH,
        )

    zz = (x * 4 + zh) * 2 + zl
    zo = lax.rem(zz + 32 + 2 * zl - 1, 32)
    outer_dev = dev(zo // 8, (zo // 2) % 4, c, zo % 2, y)
    up = dev(x, zh, c, zl, (y + 1) % 4)
    down = dev(x, zh, c, zl, (y + 3) % 4)
    sibling = dev(x, zh, 1 - c, zl, y)

    fetch = pltpu.make_async_copy(vec_hbm, vec, load)
    fetch.start()
    zrecv[:, :, 0:16] = jnp.zeros((7, 8, 16, PIECE), SENT)
    zrecv[:, :, 80:96] = jnp.zeros((7, 8, 16, PIECE), SENT)
    barrier = pltpu.get_barrier_semaphore()

    def greet(where):
        pl.semaphore_signal(barrier, inc=1, device_id=where, device_id_type=MESH)

    @pl.when(keeper)
    def _():
        me = zh * 8 + zl * 4 + y

        def greet_source(i, carry):
            other = lax.rem(me + 1 + i, 32)
            greet(dev(x, other // 8, c, (other // 4) % 2, other % 4))
            return carry

        def greet_crossing(i, carry):
            greet(dev(x, i // 2, 1 - c, i % 2, y))
            return carry

        lax.fori_loop(0, 31, greet_source, 0)
        lax.fori_loop(0, 8, greet_crossing, 0)

    @pl.when(jnp.logical_not(keeper))
    def _():
        def greet_owner(i, carry):
            greet(dev(x, i // 4, c, c, i % 4))
            return carry

        def greet_crossing(i, carry):
            greet(dev(x, i, 1 - c, 1 - c, y))
            return carry

        lax.fori_loop(0, 16, greet_owner, 0)
        lax.fori_loop(0, 4, greet_crossing, 0)
        greet(dev(x, zh, 1 - c, 1 - zl, y))
        greet(up)
        greet(down)

    for d in (1, 2, 3):
        greet(dev((x + d) % 4, zh, c, zl, y))
    greet(outer_dev)

    swap_dev = dev(x, zh, zl, c, y)
    swaps = [remote(w.at[j], u.at[j], swap_s.at[j], swap_r.at[j], swap_dev) for j in range(3)]
    pairs = [
        remote(w.at[j, :, :, 1 - c], halo.at[c, j], pair_s.at[j], pair_r.at[j], dev(x, zh, zl, 1 - c, y))
        for j in range(3)
    ]
    outers = [
        remote(u.at[j, :, :, zl], halo.at[1 - zl, j], outer_s.at[j], outer_r.at[j], outer_dev)
        for j in range(3)
    ]
    on = ((y + 2) % 4) // 2
    hop1 = [
        [
            remote(u.at[j, d, half], vn.at[d, j, half], y1_s.at[d, j, part_], y1_r.at[d, j, part_], (up, down)[d])
            for part_, half in enumerate((on, 1 - on)) for d in range(2)
        ]
        for j in range(3)
    ]
    hu = (((y + 1) % 4) // 2, ((y + 3) % 4) // 2)
    hop2 = [
        [remote(vn.at[d, j, hu[d]], vn.at[2, j, d], y2_s.at[d, j], y2_r.at[d, j], (up, down)[d]) for d in range(2)]
        for j in range(3)
    ]
    sib = [remote(it.at[c, j], it.at[c, j], sib_s.at[j], sib_r.at[j], sibling) for j in range(3)]

    def go(copies):
        for copy in copies:
            copy.start()

    def arrive(copies):
        for copy in copies:
            copy.wait_recv()

    with jax.named_scope("sort"):
        row = lax.broadcasted_iota(jnp.int32, (SB, SB), 0)
        picked = jnp.where(row == order[...][None, :], 1.0, 0.0).astype(BF16)
        src = lax.broadcasted_iota(jnp.int32, (SB, SB), 0)
        dst = lax.broadcasted_iota(jnp.int32, (SB, SB), 1)
        slot = ((dst % PIECE) // 4) * 12 + (dst // PIECE) * 4 + dst % 4
        laid = jnp.where(slot == src, 1.0, 0.0).astype(BF16)
        layout[...] = laid
        onehot = jnp.dot(picked, laid, preferred_element_type=F32).astype(BF16)
        fetch.wait()

    def sort(j, kept):
        def sort_chunk(i, carry):
            plane, q = i // 4, i % 4
            at = pl.multiple_of(i * QUARTER, QUARTER)
            got = jnp.dot(
                vec[pl.ds(at, QUARTER), :], onehot[:, j * PIECE:(j + 1) * PIECE], preferred_element_type=F32
            ).astype(BF16)
            w[j, q % 2, q // 2, plane] = got

            def keep_it():
                u[j, q % 2, q // 2, plane] = got

            pl.when(kept)(keep_it)
            return carry

        lax.fori_loop(0, 8, sort_chunk, 0)

    with jax.named_scope("sort"):
        sort(0, keeper)
    pl.semaphore_wait(barrier, jnp.where(keeper, 43, 27))

    def image(lo, hi):
        def image_chunk(i, carry):
            par, half = i // 2, i % 2
            for j in range(lo, hi):
                mine = u[j, par, half].astype(F32)
                below = mine[1] - halo[0, j, par, half].astype(F32)
                above = halo[1, j, par, half].astype(F32) - mine[0]
                both = jnp.concatenate([below, above], axis=0)
                it[c, j, par, half] = both.astype(BF16).T
            return carry

        lax.fori_loop(0, 4, image_chunk, 0)

    def wide(pieces):
        return jnp.concatenate([piece.reshape(CHUNK, PIECE) for piece in pieces], axis=1)

    def product(n, who, rows, cols):
        if n == 0:
            steps = [(s // 2, s % 2) for s in range(4)]
            right = [wide([u[j, par, half] for j in cols]) for par, half in steps]
        else:
            steps = [{1: (1, s), 2: (s, y // 2), 3: (0, s)}[n] for s in range(2)]
            right = [wide([vn[NEIGHBOURS.index(n), j, s] for j in cols]) for s in range(2)]
        left = [jnp.concatenate([it[who, i, par, half] for i in rows], axis=0) for par, half in steps]
        return jnp.dot(
            jnp.concatenate(left, axis=1), jnp.concatenate(right, axis=0), preferred_element_type=F32
        )

    def kind(t):
        if t == 0:
            return True, c, y, 0
        n, own = (t - 1) % 3 + 1, t < 4
        wraps = y + n >= 4
        matched = wraps if own else jnp.logical_not(wraps)
        zp = jnp.where(matched, c, c if own else 1 - c)
        yp = jnp.where(matched, (y + n) % 4, y)
        return matched, zp, yp, jnp.where(matched, 4 - n, 3 + n)

    def put(t, rows, cols, early):
        n = 0 if t == 0 else (t - 1) % 3 + 1
        got = product(n, c if t < 4 else 1 - c, rows, cols)
        matched = kind(t)[0]

        def tiles(swapped):
            for a, i in enumerate(rows):
                for b, j in enumerate(cols):
                    tile = got[a * PIECE:(a + 1) * PIECE, b * PIECE:(b + 1) * PIECE]
                    at = (j, i) if swapped else (i, j)
                    tile = -tile.T if swapped else tile
                    slot = TILE[at] if at in TILE else at[1] + (0 if early else 10)
                    whole[t, slot] = tile.reshape(4, 32, PIECE)
                    part[t, slot] = tile.reshape(4, 32, PIECE).astype(SENT)

        if t == 0:
            tiles(False)
            return
        pl.when(matched)(lambda: tiles(False))
        pl.when(jnp.logical_not(matched))(lambda: tiles(True))

    def xcopies(t, phase, start, length):
        run = pl.ds(start, length)
        return [
            remote(part.at[t, run, (x + d) % 4], xrecv.at[t, d - 1, run], x_s.at[t, phase, d - 1],
                   x_r.at[t, phase, d - 1], dev((x + d) % 4, zh, c, zl, y))
            for d in (1, 2, 3)
        ]

    z8 = zh * 2 + zl

    def collect(t, phase, start, length):
        arrive(xcopies(t, phase, start, length))
        run = pl.ds(start, length)
        total = whole[t, run, x]
        for d in range(3):
            total = total + xrecv[t, d, run].astype(F32)
        total = total.astype(SENT)
        rows = pl.ds(pl.multiple_of(8 * start, 16), 8 * length)
        _, zp, yp, slot = kind(t)
        here = (zp == zl) & (yp == y) & keeper
        for h in range(4):
            zsend[t, h, rows] = total[:, 8 * h:8 * h + 8].reshape(8 * length, PIECE)
            copy = remote(zsend.at[t, h, rows], zrecv.at[slot, z8, rows], z_s.at[t], z_r.at[slot], dev(x, h, zp, zp, yp))
            pl.when(jnp.logical_not(here & (zh == h)))(copy.start)

        @pl.when(here)
        def _():
            zrecv[slot, z8, rows] = zsend[t, zh, rows]

    def side(t, one, other):
        return jnp.where(kind(t)[0], one, other)

    def pass_on(j):
        for d in range(2):
            hop1[j][d].wait_recv()
            hop2[j][d].start()

    def all_here(j):
        arrive(hop1[j][2:])
        arrive(hop2[j])

    def settle(copies):
        for copy in copies:
            copy.wait_send()

    def done(runs):
        for j in range(3):
            settle([outers[j], sib[j]] + hop1[j] + hop2[j])
        for run in runs:
            settle(xcopies(*run))
        for t in range(7):
            _, zp, yp, _ = kind(t)
            here = (zp == zl) & (yp == y) & keeper

            @pl.when(here)
            def _():
                pltpu.make_async_copy(zsend.at[t, 0:3, 0:80], zsend.at[t, 0:3, 0:80], z_s.at[t]).wait()

            @pl.when(jnp.logical_not(here))
            def _():
                pltpu.make_async_copy(zsend.at[t, :, 0:80], zsend.at[t, :, 0:80], z_s.at[t]).wait()

    final = remote(fin, finr, fin_s, fin_r, sibling)

    def write(ref):
        for k in range(4):
            for j in range(3):
                rows = ref[k, j]
                out[k, 4 * j:4 * j + 4, :] = jnp.where(c == 0, rows[0:4], rows[4:8])

    def keep():
        everything = (0, 1, 2)
        pairs[0].start()
        for j in range(3):
            if j > 0:
                sort(j, True)
            go(hop1[j])
            outers[j].start()
        pairs[0].wait_send()
        pl.semaphore_signal(sent, inc=1, device_id=sibling, device_id_type=MESH)
        for j in range(3):
            pass_on(j)

        def ready(j):
            arrive([pairs[j], outers[j]])
            image(j, j + 1)
            sib[j].start()

        ready(0)
        for j in range(3):
            all_here(j)
        pl.semaphore_wait(sent, 1)
        pairs[1].start()
        ready(1)
        runs = [(t, 0, side(t, 2, 0), 6) for t in range(7)]
        rest = [(t, 1, side(t, 8, 6), 4) for t in range(7)]

        def early(t):
            put(t, (0, 1), everything, True)
            go(xcopies(*runs[t]))

        def late(t):
            put(t, (2,), everything, False)
            go(xcopies(*rest[t]))

        for t in range(4):
            early(t)
        pairs[1].wait_send()
        pairs[2].start()
        ready(2)
        for t in range(4):
            late(t)
        for t in range(4):
            collect(*runs[t])
        arrive(sib[:2])
        for t in (4, 5, 6):
            early(t)
        for t in range(4):
            collect(*rest[t])
        arrive(sib[2:])
        for t in (4, 5, 6):
            late(t)
        for t in (4, 5, 6):
            collect(*runs[t])
        for t in (4, 5, 6):
            collect(*rest[t])

        for s in range(7):
            if s == 0:
                few = y < 4
            elif s < 4:
                few = y > 4
            else:
                few = y + (s - 3) < 4

            @pl.when(few)
            def _():
                pltpu.make_async_copy(zrecv.at[s, 0:7, 0:80], zrecv.at[s, 0:7, 0:80], z_r.at[s]).wait()

            @pl.when(jnp.logical_not(few))
            def _():
                pltpu.make_async_copy(zrecv.at[s, :, 0:80], zrecv.at[s, :, 0:80], z_r.at[s]).wait()

        flats = []
        for k in range(4):
            total = jnp.sum(zrecv[k].astype(F32), axis=0)
            if k > 0:
                total = total + jnp.sum(zrecv[3 + k].astype(F32), axis=0)
            at = [total[8 * i:8 * i + 8] for i in range(12)]
            flats += [
                jnp.concatenate([at[2], at[3], at[6]], axis=1),
                jnp.concatenate([at[4], at[5], at[7]], axis=1),
                jnp.concatenate([at[0] + at[10], at[1] + at[11], at[8]], axis=1),
            ]
        flat = jnp.concatenate(flats, axis=0)
        high = flat.astype(BF16)
        left = flat - high.astype(F32)
        middle = left.astype(BF16)
        low = (left - middle.astype(F32)).astype(BF16)
        flat = lax.dot_general(
            jnp.concatenate([high, middle, low], axis=0), layout[...], (((1,), (1,)), ((), ())),
            preferred_element_type=F32,
        )
        flat = flat[0:96] + flat[96:192] + flat[192:288]
        fin[...] = flat.reshape(4, 3, 8, SB)
        final.start()
        write(fin)
        final.wait_send()
        pairs[2].wait_send()
        done(runs + rest)

    def swap():
        everything = (0, 1, 2)
        def ready(j):
            arrive([pairs[j], outers[j]])
            image(j, j + 1)
            sib[j].start()

        swaps[0].start()
        pairs[0].start()
        for j in (1, 2):
            sort(j, False)
            pairs[j].start()
        pl.semaphore_wait(sent, 1)
        swaps[1].start()
        swaps[0].wait_send()
        swaps[2].start()
        swaps[0].wait_recv()
        go(hop1[0])
        outers[0].start()
        ready(0)
        pass_on(0)
        swaps[1].wait_send()
        swaps[1].wait_recv()
        go(hop1[1])
        outers[1].start()
        pass_on(1)
        swaps[2].wait_send()
        pl.semaphore_signal(sent, inc=1, device_id=sibling, device_id_type=MESH)
        swaps[2].wait_recv()
        go(hop1[2])
        outers[2].start()
        pass_on(2)
        all_here(0)
        all_here(1)
        runs = [(t, 0, 2, 4) for t in range(4)] + [(t, 0, side(t, 0, 2), 6) for t in (4, 5, 6)]
        ready(1)
        for t in range(4):
            put(t, (0, 1), (0, 1), True)
            go(xcopies(*runs[t]))
        arrive(sib)
        for t in (4, 5, 6):
            put(t, everything, (0, 1), True)
            go(xcopies(*runs[t]))
        for t in range(4):
            collect(*runs[t])
        all_here(2)
        rest = []
        for t in (4, 5, 6):
            put(t, everything, (2,), False)
            rest.append((t, 1, side(t, 6, 8), 4))
            go(xcopies(*rest[-1]))
        ready(2)
        for t in range(4):
            put(t, (2,), everything, False)
            put(t, (0, 1), (2,), False)
            rest.append((t, 1, 6, 6))
            go(xcopies(*rest[-1]))
        for run in runs[4:] + rest:
            collect(*run)
        settle(pairs)
        done(runs + rest)
        final.wait_recv()
        write(finr)

    pl.when(keeper)(keep)
    pl.when(jnp.logical_not(keeper))(swap)


def on_device(vectors, state_order):
    dma = pltpu.SemaphoreType.DMA
    return pl.pallas_call(
        kernel,
        out_shape=jax.ShapeDtypeStruct((4, 12, SB), F32),
        in_specs=[pl.BlockSpec(memory_space=pl.ANY), pl.BlockSpec(memory_space=pltpu.VMEM)],
        out_specs=pl.BlockSpec(memory_space=pltpu.VMEM),
        scratch_shapes=[
            pltpu.VMEM((2 * PLANE, SB), BF16),
            pltpu.VMEM((3, 2, 2, 2, QUARTER, PIECE), BF16),
            pltpu.VMEM((3, 2, 2, 2, QUARTER, PIECE), BF16),
            pltpu.VMEM((2, 3, 2, 2, QUARTER, PIECE), BF16),
            pltpu.VMEM((2, 3, 2, 2, PIECE, CHUNK), BF16),
            pltpu.VMEM((3, 3, 2, 2, QUARTER, PIECE), BF16),
            pltpu.VMEM((7, 12, 4, 32, PIECE), F32),
            pltpu.VMEM((7, 12, 4, 32, PIECE), SENT),
            pltpu.VMEM((7, 3, 12, 32, PIECE), SENT),
            pltpu.VMEM((7, 4, 96, PIECE), SENT),
            pltpu.VMEM((7, 8, 96, PIECE), SENT),
            pltpu.VMEM((4, 3, 8, SB), F32),
            pltpu.VMEM((4, 3, 8, SB), F32),
            pltpu.VMEM((SB, SB), BF16),
            dma((3,)), dma((3,)), dma((3,)), dma((3,)), dma((3,)), dma((3,)),
            dma((3,)), dma((3,)),
            dma((2, 3, 2)), dma((2, 3, 2)), dma((2, 3)), dma((2, 3)),
            dma((7, 3, 3)), dma((7, 3, 3)), dma((7,)), dma((7,)),
            dma, dma, dma, pltpu.SemaphoreType.REGULAR,
        ],
        compiler_params=pltpu.CompilerParams(
            collective_id=0, has_side_effects=True, vmem_limit_bytes=60 * 1024 * 1024
        ),
        cost_estimate=pl.CostEstimate(flops=6_000_000_000, bytes_accessed=4_000_000, transcendentals=0),
    )(vectors, state_order)


def solution(mesh):
    return jax.shard_map(
        on_device,
        mesh=mesh,
        in_specs=(P("slab", "blk"), P("blk")),
        out_specs=P(None, "slab", "blk"),
        check_vma=False,
    )
```

```python
import jax
import jax.numpy as jnp
from jax import lax
from jax.experimental import pallas as pl
from jax.experimental.pallas import tpu as pltpu
from jax.sharding import PartitionSpec as P

PLANE = 2304
QUARTER = 576
CHUNK = 1152
SB = 384
PIECE = 128
BF16 = jnp.bfloat16
F32 = jnp.float32
SENT = jnp.bfloat16
MESH = pl.DeviceIdType.MESH
NEIGHBOURS = (3, 1, 2)
TILE = {(0, 0): 2, (0, 1): 3, (1, 0): 4, (1, 1): 5, (0, 2): 6, (1, 2): 7, (2, 2): 8}


def kernel(
    vec_hbm, order, out,
    vec, w, u, halo, it, vn, whole, part, xrecv, zsend, zrecv, fin, finr, layout,
    swap_s, swap_r, pair_s, pair_r, outer_s, outer_r, sib_s, sib_r,
    y1_s, y1_r, y2_s, y2_r, x_s, x_r, z_s, z_r, fin_s, fin_r, load, sent,
):
    slab, blk = lax.axis_index("slab"), lax.axis_index("blk")
    x, zh, c = slab // 8, (slab // 2) % 4, slab % 2
    zl, y = blk // 4, blk % 4
    keeper = c == zl

    def dev(x_, zh_, c_, zl_, y_):
        return (x_ * 8 + zh_ * 2 + c_, zl_ * 4 + y_)

    def remote(src, dst, ss, rs, where):
        return pltpu.make_async_remote_copy(
            src_ref=src, dst_ref=dst, send_sem=ss, recv_sem=rs,
            device_id=where, device_id_type=MESH,
        )

    zz = (x * 4 + zh) * 2 + zl
    zo = lax.rem(zz + 32 + 2 * zl - 1, 32)
    outer_dev = dev(zo // 8, (zo // 2) % 4, c, zo % 2, y)
    up = dev(x, zh, c, zl, (y + 1) % 4)
    down = dev(x, zh, c, zl, (y + 3) % 4)
    sibling = dev(x, zh, 1 - c, zl, y)

    fetch = [
        pltpu.make_async_copy(vec_hbm.at[pl.ds(f * CHUNK, CHUNK)], vec.at[pl.ds(f * CHUNK, CHUNK)], load.at[f])
        for f in range(4)
    ]
    for copy in fetch:
        copy.start()
    zrecv[:, :, 0:16] = jnp.zeros((7, 8, 16, PIECE), SENT)
    zrecv[:, :, 80:96] = jnp.zeros((7, 8, 16, PIECE), SENT)
    barrier = pltpu.get_barrier_semaphore()

    def greet(where):
        pl.semaphore_signal(barrier, inc=1, device_id=where, device_id_type=MESH)

    @pl.when(keeper)
    def _():
        me = zh * 8 + zl * 4 + y

        def greet_source(i, carry):
            other = lax.rem(me + 1 + i, 32)
            greet(dev(x, other // 8, c, (other // 4) % 2, other % 4))
            return carry

        def greet_crossing(i, carry):
            greet(dev(x, i // 2, 1 - c, i % 2, y))
            return carry

        lax.fori_loop(0, 31, greet_source, 0)
        lax.fori_loop(0, 8, greet_crossing, 0)

    @pl.when(jnp.logical_not(keeper))
    def _():
        def greet_owner(i, carry):
            greet(dev(x, i // 4, c, c, i % 4))
            return carry

        def greet_crossing(i, carry):
            greet(dev(x, i, 1 - c, 1 - c, y))
            return carry

        lax.fori_loop(0, 16, greet_owner, 0)
        lax.fori_loop(0, 4, greet_crossing, 0)
        greet(dev(x, zh, 1 - c, 1 - zl, y))
        greet(up)
        greet(down)

    for d in (1, 2, 3):
        greet(dev((x + d) % 4, zh, c, zl, y))
    greet(outer_dev)

    swap_dev = dev(x, zh, zl, c, y)
    swaps = [remote(w.at[j], u.at[j], swap_s.at[j], swap_r.at[j], swap_dev) for j in range(3)]
    pairs = [
        remote(w.at[j, :, :, 1 - c], halo.at[c, j], pair_s.at[j], pair_r.at[j], dev(x, zh, zl, 1 - c, y))
        for j in range(3)
    ]
    outers = [
        remote(u.at[j, :, :, zl], halo.at[1 - zl, j], outer_s.at[j], outer_r.at[j], outer_dev)
        for j in range(3)
    ]
    on = ((y + 2) % 4) // 2
    hop1 = [
        [
            remote(u.at[j, d, half], vn.at[d, j, half], y1_s.at[d, j, part_], y1_r.at[d, j, part_], (up, down)[d])
            for part_, half in enumerate((on, 1 - on)) for d in range(2)
        ]
        for j in range(3)
    ]
    hu = (((y + 1) % 4) // 2, ((y + 3) % 4) // 2)
    hop2 = [
        [remote(vn.at[d, j, hu[d]], vn.at[2, j, d], y2_s.at[d, j], y2_r.at[d, j], (up, down)[d]) for d in range(2)]
        for j in range(3)
    ]
    sib = [remote(it.at[c, j], it.at[c, j], sib_s.at[j], sib_r.at[j], sibling) for j in range(3)]

    def go(copies):
        for copy in copies:
            copy.start()

    def arrive(copies):
        for copy in copies:
            copy.wait_recv()

    with jax.named_scope("sort"):
        row = lax.broadcasted_iota(jnp.int32, (SB, SB), 0)
        picked = jnp.where(row == order[...][None, :], 1.0, 0.0).astype(BF16)
        src = lax.broadcasted_iota(jnp.int32, (SB, SB), 0)
        dst = lax.broadcasted_iota(jnp.int32, (SB, SB), 1)
        slot = ((dst % PIECE) // 4) * 12 + (dst // PIECE) * 4 + dst % 4
        laid = jnp.where(slot == src, 1.0, 0.0).astype(BF16)
        layout[...] = laid
        onehot = jnp.dot(picked, laid, preferred_element_type=F32).astype(BF16)

    def sort(j, kept):
        def sort_chunk(i, carry):
            plane, q = i // 4, i % 4
            at = pl.multiple_of(i * QUARTER, QUARTER)
            got = jnp.dot(
                vec[pl.ds(at, QUARTER), :], onehot[:, j * PIECE:(j + 1) * PIECE], preferred_element_type=F32
            ).astype(BF16)
            w[j, q % 2, q // 2, plane] = got

            def keep_it():
                u[j, q % 2, q // 2, plane] = got

            pl.when(kept)(keep_it)
            return carry

        for f in range(4):
            if j == 0:
                fetch[f].wait()
            lax.fori_loop(2 * f, 2 * f + 2, sort_chunk, 0)

    with jax.named_scope("sort"):
        sort(0, keeper)
    pl.semaphore_wait(barrier, jnp.where(keeper, 43, 27))

    def image(lo, hi):
        def image_chunk(i, carry):
            par, half = i // 2, i % 2
            for j in range(lo, hi):
                mine = u[j, par, half].astype(F32)
                below = mine[1] - halo[0, j, par, half].astype(F32)
                above = halo[1, j, par, half].astype(F32) - mine[0]
                both = jnp.concatenate([below, above], axis=0)
                it[c, j, par, half] = both.astype(BF16).T
            return carry

        lax.fori_loop(0, 4, image_chunk, 0)

    def wide(pieces):
        return jnp.concatenate([piece.reshape(CHUNK, PIECE) for piece in pieces], axis=1)

    def product(n, who, rows, cols):
        if n == 0:
            steps = [(s // 2, s % 2) for s in range(4)]
            right = [wide([u[j, par, half] for j in cols]) for par, half in steps]
        else:
            steps = [{1: (1, s), 2: (s, y // 2), 3: (0, s)}[n] for s in range(2)]
            right = [wide([vn[NEIGHBOURS.index(n), j, s] for j in cols]) for s in range(2)]
        left = [jnp.concatenate([it[who, i, par, half] for i in rows], axis=0) for par, half in steps]
        return jnp.dot(
            jnp.concatenate(left, axis=1), jnp.concatenate(right, axis=0), preferred_element_type=F32
        )

    def kind(t):
        if t == 0:
            return True, c, y, 0
        n, own = (t - 1) % 3 + 1, t < 4
        wraps = y + n >= 4
        matched = wraps if own else jnp.logical_not(wraps)
        zp = jnp.where(matched, c, c if own else 1 - c)
        yp = jnp.where(matched, (y + n) % 4, y)
        return matched, zp, yp, jnp.where(matched, 4 - n, 3 + n)

    def put(t, rows, cols, early):
        n = 0 if t == 0 else (t - 1) % 3 + 1
        got = product(n, c if t < 4 else 1 - c, rows, cols)
        matched = kind(t)[0]

        def tiles(swapped):
            for a, i in enumerate(rows):
                for b, j in enumerate(cols):
                    tile = got[a * PIECE:(a + 1) * PIECE, b * PIECE:(b + 1) * PIECE]
                    at = (j, i) if swapped else (i, j)
                    tile = -tile.T if swapped else tile
                    slot = TILE[at] if at in TILE else at[1] + (0 if early else 10)
                    whole[t, slot] = tile.reshape(4, 32, PIECE)
                    part[t, slot] = tile.reshape(4, 32, PIECE).astype(SENT)

        if t == 0:
            tiles(False)
            return
        pl.when(matched)(lambda: tiles(False))
        pl.when(jnp.logical_not(matched))(lambda: tiles(True))

    def xcopies(t, phase, start, length):
        run = pl.ds(start, length)
        return [
            remote(part.at[t, run, (x + d) % 4], xrecv.at[t, d - 1, run], x_s.at[t, phase, d - 1],
                   x_r.at[t, phase, d - 1], dev((x + d) % 4, zh, c, zl, y))
            for d in (1, 2, 3)
        ]

    z8 = zh * 2 + zl

    def collect(t, phase, start, length):
        arrive(xcopies(t, phase, start, length))
        run = pl.ds(start, length)
        total = whole[t, run, x]
        for d in range(3):
            total = total + xrecv[t, d, run].astype(F32)
        total = total.astype(SENT)
        rows = pl.ds(pl.multiple_of(8 * start, 16), 8 * length)
        _, zp, yp, slot = kind(t)
        here = (zp == zl) & (yp == y) & keeper
        for h in range(4):
            zsend[t, h, rows] = total[:, 8 * h:8 * h + 8].reshape(8 * length, PIECE)
            copy = remote(zsend.at[t, h, rows], zrecv.at[slot, z8, rows], z_s.at[t], z_r.at[slot], dev(x, h, zp, zp, yp))
            pl.when(jnp.logical_not(here & (zh == h)))(copy.start)

        @pl.when(here)
        def _():
            zrecv[slot, z8, rows] = zsend[t, zh, rows]

    def side(t, one, other):
        return jnp.where(kind(t)[0], one, other)

    def pass_on(j):
        for d in range(2):
            hop1[j][d].wait_recv()
            hop2[j][d].start()

    def all_here(j):
        arrive(hop1[j][2:])
        arrive(hop2[j])

    def settle(copies):
        for copy in copies:
            copy.wait_send()

    def done(runs):
        for j in range(3):
            settle([outers[j], sib[j]] + hop1[j] + hop2[j])
        for run in runs:
            settle(xcopies(*run))
        for t in range(7):
            _, zp, yp, _ = kind(t)
            here = (zp == zl) & (yp == y) & keeper

            @pl.when(here)
            def _():
                pltpu.make_async_copy(zsend.at[t, 0:3, 0:80], zsend.at[t, 0:3, 0:80], z_s.at[t]).wait()

            @pl.when(jnp.logical_not(here))
            def _():
                pltpu.make_async_copy(zsend.at[t, :, 0:80], zsend.at[t, :, 0:80], z_s.at[t]).wait()

    final = remote(fin, finr, fin_s, fin_r, sibling)

    def write(ref):
        for k in range(4):
            for j in range(3):
                rows = ref[k, j]
                out[k, 4 * j:4 * j + 4, :] = jnp.where(c == 0, rows[0:4], rows[4:8])

    def keep():
        everything = (0, 1, 2)
        pairs[0].start()
        for j in range(3):
            if j > 0:
                sort(j, True)
            go(hop1[j])
            outers[j].start()
        pairs[0].wait_send()
        pl.semaphore_signal(sent, inc=1, device_id=sibling, device_id_type=MESH)
        for j in range(3):
            pass_on(j)

        def ready(j):
            arrive([pairs[j], outers[j]])
            image(j, j + 1)
            sib[j].start()

        ready(0)
        for j in range(3):
            all_here(j)
        pl.semaphore_wait(sent, 1)
        pairs[1].start()
        ready(1)
        runs = [(t, 0, side(t, 2, 0), 6) for t in range(7)]
        rest = [(t, 1, side(t, 8, 6), 4) for t in range(7)]

        def early(t):
            put(t, (0, 1), everything, True)
            go(xcopies(*runs[t]))

        def late(t):
            put(t, (2,), everything, False)
            go(xcopies(*rest[t]))

        for t in range(4):
            early(t)
        pairs[1].wait_send()
        pairs[2].start()
        ready(2)
        for t in range(4):
            late(t)
        for t in range(4):
            collect(*runs[t])
        arrive(sib[:2])
        for t in (4, 5, 6):
            early(t)
        for t in range(4):
            collect(*rest[t])
        arrive(sib[2:])
        for t in (4, 5, 6):
            late(t)
        for t in (4, 5, 6):
            collect(*runs[t])
        for t in (4, 5, 6):
            collect(*rest[t])

        for s in range(7):
            if s == 0:
                few = y < 4
            elif s < 4:
                few = y > 4
            else:
                few = y + (s - 3) < 4

            @pl.when(few)
            def _():
                pltpu.make_async_copy(zrecv.at[s, 0:7, 0:80], zrecv.at[s, 0:7, 0:80], z_r.at[s]).wait()

            @pl.when(jnp.logical_not(few))
            def _():
                pltpu.make_async_copy(zrecv.at[s, :, 0:80], zrecv.at[s, :, 0:80], z_r.at[s]).wait()

        flats = []
        for k in range(4):
            total = jnp.sum(zrecv[k].astype(F32), axis=0)
            if k > 0:
                total = total + jnp.sum(zrecv[3 + k].astype(F32), axis=0)
            at = [total[8 * i:8 * i + 8] for i in range(12)]
            flats += [
                jnp.concatenate([at[2], at[3], at[6]], axis=1),
                jnp.concatenate([at[4], at[5], at[7]], axis=1),
                jnp.concatenate([at[0] + at[10], at[1] + at[11], at[8]], axis=1),
            ]
        flat = jnp.concatenate(flats, axis=0)
        high = flat.astype(BF16)
        left = flat - high.astype(F32)
        middle = left.astype(BF16)
        low = (left - middle.astype(F32)).astype(BF16)
        flat = lax.dot_general(
            jnp.concatenate([high, middle, low], axis=0), layout[...], (((1,), (1,)), ((), ())),
            preferred_element_type=F32,
        )
        flat = flat[0:96] + flat[96:192] + flat[192:288]
        fin[...] = flat.reshape(4, 3, 8, SB)
        final.start()
        write(fin)
        final.wait_send()
        pairs[2].wait_send()
        done(runs + rest)

    def swap():
        everything = (0, 1, 2)
        def ready(j):
            arrive([pairs[j], outers[j]])
            image(j, j + 1)
            sib[j].start()

        swaps[0].start()
        pairs[0].start()
        for j in (1, 2):
            sort(j, False)
            pairs[j].start()
        pl.semaphore_wait(sent, 1)
        swaps[1].start()
        swaps[0].wait_send()
        swaps[2].start()
        swaps[0].wait_recv()
        go(hop1[0])
        outers[0].start()
        ready(0)
        pass_on(0)
        swaps[1].wait_send()
        swaps[1].wait_recv()
        go(hop1[1])
        outers[1].start()
        pass_on(1)
        swaps[2].wait_send()
        pl.semaphore_signal(sent, inc=1, device_id=sibling, device_id_type=MESH)
        swaps[2].wait_recv()
        go(hop1[2])
        outers[2].start()
        pass_on(2)
        all_here(0)
        all_here(1)
        runs = [(t, 0, 2, 4) for t in range(4)] + [(t, 0, side(t, 0, 2), 6) for t in (4, 5, 6)]
        ready(1)
        for t in range(4):
            put(t, (0, 1), (0, 1), True)
            go(xcopies(*runs[t]))
        arrive(sib)
        for t in (4, 5, 6):
            put(t, everything, (0, 1), True)
            go(xcopies(*runs[t]))
        for t in range(4):
            collect(*runs[t])
        all_here(2)
        rest = []
        for t in (4, 5, 6):
            put(t, everything, (2,), False)
            rest.append((t, 1, side(t, 6, 8), 4))
            go(xcopies(*rest[-1]))
        ready(2)
        for t in range(4):
            put(t, (2,), everything, False)
            put(t, (0, 1), (2,), False)
            rest.append((t, 1, 6, 6))
            go(xcopies(*rest[-1]))
        for run in runs[4:] + rest:
            collect(*run)
        settle(pairs)
        done(runs + rest)
        final.wait_recv()
        write(finr)

    pl.when(keeper)(keep)
    pl.when(jnp.logical_not(keeper))(swap)


def on_device(vectors, state_order):
    dma = pltpu.SemaphoreType.DMA
    return pl.pallas_call(
        kernel,
        out_shape=jax.ShapeDtypeStruct((4, 12, SB), F32),
        in_specs=[pl.BlockSpec(memory_space=pl.ANY), pl.BlockSpec(memory_space=pltpu.VMEM)],
        out_specs=pl.BlockSpec(memory_space=pltpu.VMEM),
        scratch_shapes=[
            pltpu.VMEM((2 * PLANE, SB), BF16),
            pltpu.VMEM((3, 2, 2, 2, QUARTER, PIECE), BF16),
            pltpu.VMEM((3, 2, 2, 2, QUARTER, PIECE), BF16),
            pltpu.VMEM((2, 3, 2, 2, QUARTER, PIECE), BF16),
            pltpu.VMEM((2, 3, 2, 2, PIECE, CHUNK), BF16),
            pltpu.VMEM((3, 3, 2, 2, QUARTER, PIECE), BF16),
            pltpu.VMEM((7, 12, 4, 32, PIECE), F32),
            pltpu.VMEM((7, 12, 4, 32, PIECE), SENT),
            pltpu.VMEM((7, 3, 12, 32, PIECE), SENT),
            pltpu.VMEM((7, 4, 96, PIECE), SENT),
            pltpu.VMEM((7, 8, 96, PIECE), SENT),
            pltpu.VMEM((4, 3, 8, SB), F32),
            pltpu.VMEM((4, 3, 8, SB), F32),
            pltpu.VMEM((SB, SB), BF16),
            dma((3,)), dma((3,)), dma((3,)), dma((3,)), dma((3,)), dma((3,)),
            dma((3,)), dma((3,)),
            dma((2, 3, 2)), dma((2, 3, 2)), dma((2, 3)), dma((2, 3)),
            dma((7, 3, 3)), dma((7, 3, 3)), dma((7,)), dma((7,)),
            dma, dma, dma((4,)), pltpu.SemaphoreType.REGULAR,
        ],
        compiler_params=pltpu.CompilerParams(
            collective_id=0, has_side_effects=True, vmem_limit_bytes=60 * 1024 * 1024
        ),
        cost_estimate=pl.CostEstimate(flops=6_000_000_000, bytes_accessed=4_000_000, transcendentals=0),
    )(vectors, state_order)


def solution(mesh):
    return jax.shard_map(
        on_device,
        mesh=mesh,
        in_specs=(P("slab", "blk"), P("blk")),
        out_specs=P(None, "slab", "blk"),
        check_vma=False,
    )
```
